32 devices in a mesh: lat: 8 (over y, x, core), lon: 4 (over z).
Axes of the slice: x: 2, y: 2, z: 4, core: 2. Of those that a mesh axis runs over, the one named last changes fastest.
Arguments:
- fields: bfloat16 [192, 512, 128], P('lat', 'lon'), may hold values from -6 to 6
- req_block: int32 [8, 4, 3, 1280], P('lat', 'lon'), may hold values from 0 to 191
- req_stencil: int32 [8, 4, 3, 4, 1280], P('lat', 'lon'), may hold values from 0 to 15
- req_frac: int32 [8, 4, 3, 2, 1280], P('lat', 'lon'), may hold values from 0 to 15
- req_count: int32 [8, 4, 3], P('lat', 'lon'), may hold values from 597 to 1280, as said below
- legendre: bfloat16 [1536, 192, 768], P(('lon', 'lat')), may hold values from -0.4375 to 0.4375
Outputs:
- spectral: float32 [1536, 768, 128], P(('lon', 'lat'))
The draws below stay inside these ranges and needn't reach their ends.
Inputs may be any that keep to these rules, and one draw needn't show every extreme that they name: `req_count`: the three counts of a tile sum to 3072; positions j at or beyond a slot's count are unused. In every latitude band some tile receives 1280 points from each of the three tiles whose slots reach it, and every tile fills one slot to 1280.
All inputs are finite; a program needn't handle non-finite values.
Results may differ from the reference program's by a relative error of at most 0.0048.
Values may be sent and summed in bfloat16 or wider, within the bound.
No kernel may reach another device: no remote copies, remote signals or barrier semaphores. Data moves between devices by JAX's collectives and lax.ppermute only.
A program may use at most 128 MiB of HBM per device.

```python
import math
import jax
import jax.numpy as jnp
from jax import lax

CHANNELS = 128
LAT_DEV = 24
LON_DEV = 128
KF = 1536
NN = 768
BLK = 16
FRAC = 16
COLS = 3072
CAP = 1280
NLAT = 192
NLON = 512
N_LAT = 8
N_LON = 4


def draw_req_count(key, part):
    key_hot = jax.random.fold_in(key, 11)
    key_jet = jax.random.fold_in(key, 23)
    key_share = jax.random.fold_in(key, 37)
    hot_sector = jax.random.randint(key_hot, (N_LAT, 1), 0, N_LON)
    source = jnp.arange(N_LON, dtype=jnp.int32)[None, :]
    toward_hot = (hot_sector - source + 1) % N_LON
    jet_slot = jax.random.randint(key_jet, (N_LAT, N_LON), 0, 3)
    full_slot = jnp.where(toward_hot <= 2, toward_hot, jet_slot)
    slot_index = jnp.arange(3, dtype=jnp.int32)[None, None, :]
    is_full = slot_index == full_slot[:, :, None]
    weights = jax.random.randint(key_share, (N_LAT, N_LON, 3), 2, 5)
    weights = jnp.where(is_full, 0, weights)
    remaining = COLS - CAP
    shares = remaining * weights // jnp.sum(weights, axis=2, keepdims=True)
    leftover = remaining - jnp.sum(shares, axis=2, keepdims=True)
    first_other = jnp.where(full_slot == 0, 1, 0)
    shares = shares + jnp.where(slot_index == first_other[:, :, None], leftover, 0)
    return jnp.where(is_full, CAP, shares).astype(jnp.int32)


def set_ends(array, stream_key, smallest, top_value):
    spot = [jax.random.randint(jax.random.fold_in(stream_key, axis), (), 0, length) for axis, length in enumerate(array.shape)]
    widest = array.shape.index(max(array.shape))
    beside = spot[:widest] + [(spot[widest] + 1) % array.shape[widest]] + spot[widest + 1:]
    return array.at[tuple(spot)].set(smallest).at[tuple(beside)].set(top_value)


def shard_levels(rng, shape, cuts, least, high):
    loudness = 1.0
    for position, parts in cuts:
        steps = jax.random.uniform(jax.random.fold_in(jax.random.fold_in(rng, 6), position), (parts,), jnp.float32, least / len(cuts), high / len(cuts))
        loudness = loudness * jnp.repeat(jnp.exp(steps), shape[position] // parts).reshape((-1,) + (1,) * (len(shape) - 1 - position))
    return loudness


def noise(own_key, dims, scale, bound, split=(), held_as=jnp.bfloat16):
    entries = scale * jax.random.normal(own_key, dims, jnp.float32)
    if split:
        entries = entries * shard_levels(own_key, dims, split, -0.22, 0.18)
    return jnp.clip(entries, -bound, bound).astype(held_as)


def setup_inputs(seed: int = 0) -> dict:
    keys = jax.random.split(jax.random.key(seed), 7)
    fields = noise(keys[0], (NLAT, NLON, CHANNELS), 1.0, 6.0, ((0, 8), (1, 4)))
    req_block = set_ends(jax.random.randint(keys[1], (NLAT // LAT_DEV, NLON // LON_DEV, 3, CAP), 0, COLS // BLK), jax.random.fold_in(keys[1], 1), 0, (COLS // BLK) - 1).astype(jnp.int32)
    req_stencil = set_ends(jax.random.randint(keys[2], (NLAT // LAT_DEV, NLON // LON_DEV, 3, 4, CAP), 0, BLK), jax.random.fold_in(keys[2], 1), 0, BLK - 1).astype(jnp.int32)
    req_frac = set_ends(jax.random.randint(keys[3], (NLAT // LAT_DEV, NLON // LON_DEV, 3, 2, CAP), 0, FRAC), jax.random.fold_in(keys[3], 1), 0, FRAC - 1).astype(jnp.int32)
    req_count = draw_req_count(jax.random.fold_in(keys[6], 71), 0)
    legendre = noise(keys[5], (KF, NLAT, NN), NLAT ** -0.5, 0.4375, ((0, 32),))
    return {"fields": fields, "req_block": req_block, "req_stencil": req_stencil, "req_frac": req_frac, "req_count": req_count, "legendre": legendre}


def hartley_table(lon_total):
    wave_index = jnp.arange(KF, dtype=jnp.int32)
    lon_index = jnp.arange(lon_total, dtype=jnp.int32)
    phase_index = wave_index[:, None] * lon_index[None, :] % lon_total
    phase_angle = 2.0 * math.pi / lon_total * phase_index.astype(jnp.float32)
    return ((jnp.cos(phase_angle) + jnp.sin(phase_angle)) / math.sqrt(lon_total)).astype(jnp.bfloat16)

def interpolate(own_tile, packed):
    cell_rows = (packed[0][None, :] * BLK + packed[1:5]).astype(jnp.int32)
    picked = jnp.take(own_tile, cell_rows.reshape(-1), axis=0).astype(jnp.float32)
    picked = picked.reshape(4, cell_rows.shape[1], own_tile.shape[1])
    frac_lat = (packed[5].astype(jnp.float32) + 0.5) / FRAC
    frac_lon = (packed[6].astype(jnp.float32) + 0.5) / FRAC
    weights = jnp.stack([(1.0 - frac_lat) * (1.0 - frac_lon), frac_lat * (1.0 - frac_lon), (1.0 - frac_lat) * frac_lon, frac_lat * frac_lon])
    return lax.optimization_barrier(jnp.sum(weights[:, :, None] * picked, axis=0)).astype(jnp.bfloat16)

def place_columns(values, counts):
    slot_ends = jnp.cumsum(counts).astype(jnp.int32)
    starts = slot_ends - counts
    column = jnp.arange(COLS, dtype=jnp.int32)
    slot_index = lax.optimization_barrier(jnp.sum((slot_ends[None, :] <= column[:, None]).astype(jnp.int32), axis=1))
    onehot = slot_index[:, None] == jnp.arange(3, dtype=jnp.int32)[None, :]
    offset = column - lax.optimization_barrier(jnp.sum(jnp.where(onehot, starts[None, :], 0), axis=1)).astype(jnp.int32)
    flat_index = (slot_index * values.shape[1] + offset).astype(jnp.int32)
    return jnp.take(values.reshape(-1, values.shape[-1]), flat_index, axis=0)

def reference(fields, req_block, req_stencil, req_frac, req_count, legendre):
    lon_total = LON_DEV * N_LON
    lat_total = LAT_DEV * N_LAT
    all_tiles = fields.reshape(N_LAT, LAT_DEV, N_LON, LON_DEV, CHANNELS).transpose(0, 2, 1, 3, 4)
    all_tiles = all_tiles.reshape(N_LAT, N_LON, COLS, CHANNELS)
    packed = jnp.concatenate([req_block[:, :, :, None, :], req_stencil, req_frac], axis=3)
    hartley = hartley_table(lon_total).astype(jnp.float32)

    def one_band(inputs):
        band_tiles, band_packed, band_count = inputs

        def one_source(source):
            slot_values = []
            for slot_index in range(3):
                owner = (source + slot_index - 1) % N_LON
                slot_values.append(interpolate(band_tiles[owner], band_packed[source, slot_index]))
            return place_columns(jnp.stack(slot_values), band_count[source])
        departed = jax.vmap(one_source)(jnp.arange(N_LON, dtype=jnp.int32))
        band_grid = departed.reshape(N_LON, LAT_DEV, LON_DEV, CHANNELS).transpose(1, 0, 2, 3)
        band_grid = band_grid.reshape(LAT_DEV, lon_total, CHANNELS).astype(jnp.float32)
        fourier = jnp.einsum('kx,yxc->ykc', hartley, band_grid)
        return fourier.astype(jnp.bfloat16)
    fourier = lax.map(one_band, (all_tiles, packed, req_count)).reshape(lat_total, KF, CHANNELS)
    blocks = KF // 64
    leg_blocks = legendre.reshape(blocks, 64, lat_total, NN)
    four_blocks = fourier.reshape(lat_total, blocks, 64, CHANNELS).transpose(1, 0, 2, 3)

    def project(inputs):
        leg_block, four_block = inputs
        return jnp.einsum('kyn,ykc->knc', leg_block.astype(jnp.float32), four_block.astype(jnp.float32))
    projected = lax.map(project, (leg_blocks, four_blocks)).reshape(KF, NN, CHANNELS)
    degree = jnp.arange(NN, dtype=jnp.float32)
    factor = 1.0 / (1.0 + 4.0 * degree * (degree + 1.0) / (NN * (NN + 1)))
    return projected * factor[None, :, None]
```

```python
import functools
import math

import jax
import jax.numpy as jnp
from jax import lax
from jax.experimental import pallas as pl
from jax.experimental.pallas import tpu as pltpu
from jax.sharding import PartitionSpec as P

BLK = 16
FRAC = 16
SLOTS = 3
LANES = 128
SPAN = 2 * LANES
F32 = jnp.float32
BF16 = jnp.bfloat16


def hartley_table(waves, lon_total):
    wave_index = jnp.arange(waves, dtype=jnp.int32)
    lon_index = jnp.arange(lon_total, dtype=jnp.int32)
    phase_index = wave_index[:, None] * lon_index[None, :] % lon_total
    phase_angle = 2.0 * math.pi / lon_total * phase_index.astype(F32)
    return ((jnp.cos(phase_angle) + jnp.sin(phase_angle)) / math.sqrt(lon_total)).astype(BF16)


def chunk_list(channels):
    half = channels // 2
    return ((0, half), (half, half // 2), (half + half // 2, half // 2))


def pack_body(chunks, blocks, counts, fields, block, stencil, frac, *rest):
    outs, wide = rest[:-1], rest[-1]
    cells = blocks * BLK
    cap = block.shape[1]
    wide[...] = fields[...].astype(F32)
    lane = lax.broadcasted_iota(jnp.int32, (blocks, LANES), 1)
    for out, (first, width) in zip(outs, chunks, strict=True):
        groups = LANES // width
        planes = BLK // groups
        for plane in range(planes):
            total = None
            for group in range(groups):
                rows = wide[pl.ds(group * planes + plane, blocks, stride=BLK), :]
                shift = (group * width - first) % LANES
                if shift:
                    rows = pltpu.roll(rows, shift, 1)
                total = rows if total is None else jnp.where(lane >= group * width, rows, total)
            out[plane * blocks : (plane + 1) * blocks, :] = total.astype(BF16)
    starts = (0, counts[0], counts[0] + counts[1])
    column = lax.broadcasted_iota(jnp.int32, (8, cells), 1)
    row = lax.broadcasted_iota(jnp.int32, (8, cells), 0)
    slot = (column >= starts[1]).astype(jnp.int32) + (column >= starts[2]).astype(jnp.int32)
    placed = slot.astype(F32)
    for index in range(SLOTS):
        listed = jnp.concatenate(
            [
                block[index : index + 1, :].astype(F32),
                stencil[index].astype(F32),
                frac[index].astype(F32),
                jnp.zeros((1, cap), F32),
            ],
            axis=0,
        )
        listed = jnp.concatenate([listed, jnp.zeros((8, cells - cap), F32)], axis=1)
        if index:
            listed = pltpu.roll(listed, starts[index], 1)
        placed = jnp.where((slot == index) & (row < 7), listed, placed)
    base = outs[0].shape[0] - cells // LANES * 8
    for span in range(cells // SPAN):
        pair = jnp.concatenate(
            [
                placed[:, span * SPAN : span * SPAN + LANES],
                placed[:, span * SPAN + LANES : (span + 1) * SPAN],
            ],
            axis=0,
        )
        outs[0][base + span * 16 : base + (span + 1) * 16, :] = pair.astype(BF16)


def interp_body(count, width, blocks, lead, here, *rest):
    if lead:
        tiles, (table, out, params, ends, flipped, grid) = rest[: 2 * count - 1], rest[2 * count - 1 :]
    else:
        ends, params, *rest = rest
        tiles, (table, out, flipped, grid) = rest[: 2 * count - 1], rest[2 * count - 1 :]
    me = here[0]
    groups = LANES // width
    planes = BLK // groups
    spans = blocks * BLK // SPAN

    def take(tile, owner):
        for plane in range(planes):
            rows = tile[plane * blocks : (plane + 1) * blocks, :]
            flipped[owner, plane * LANES : (plane + 1) * LANES, :] = rows.T
        if lead:
            params[owner] = tile[planes * blocks :, :]

    take(tiles[0], me)
    for away in range(1, count):

        @pl.when(me >= away)
        def _(away=away):
            take(tiles[away], me - away)

        @pl.when(me + away < count)
        def _(away=away):
            take(tiles[count - 1 + away], me + away)

    if lead:
        for tile in range(count):
            rows = params[tile].astype(F32)
            which = lax.broadcasted_iota(jnp.int32, rows.shape, 0) % 8 == 7
            ends[tile, 0] = 0
            for index in range(SLOTS):
                listed = jnp.where(which & (rows <= index), 1.0, 0.0)
                ends[tile, index + 1] = jnp.sum(listed).astype(jnp.int32)

    grid[...] = jnp.zeros_like(grid)
    block_row = lax.broadcasted_iota(jnp.int32, (blocks, SPAN), 0).astype(F32)
    cell_row = lax.broadcasted_iota(jnp.int32, (BLK, SPAN), 0).astype(F32)

    def job(number, _):
        owner = number // SLOTS
        index = number % SLOTS
        target = lax.rem(owner - index + 1 + count, count)
        low = ends[target, index]
        high = ends[target, index + 1]
        place = pl.multiple_of(target * LANES, LANES)

        def span_step(span, _):
            both = params[target, pl.ds(pl.multiple_of(span * 16, 16), 16), :].astype(F32)

            def line(i):
                return jnp.concatenate([both[i : i + 1, :], both[8 + i : 9 + i, :]], axis=1)

            key = jnp.where(line(7) == index.astype(F32), line(0), -1.0)
            onehot = jnp.where(block_row == key, 1.0, 0.0).astype(BF16)
            f_lat = (line(5) + 0.5) / FRAC
            f_lon = (line(6) + 0.5) / FRAC
            corners = (
                (1.0 - f_lat) * (1.0 - f_lon),
                f_lat * (1.0 - f_lon),
                (1.0 - f_lat) * f_lon,
                f_lat * f_lon,
            )
            weight = jnp.zeros((BLK, SPAN), F32)
            for corner in range(4):
                weight += jnp.where(cell_row == line(1 + corner), corners[corner], 0.0)
            total = jnp.zeros((width, SPAN), F32)
            for plane in range(planes):
                picked = jnp.dot(
                    flipped[owner, plane * LANES : (plane + 1) * LANES, :],
                    onehot,
                    preferred_element_type=F32,
                )
                for group in range(groups):
                    cell = group * planes + plane
                    total += (
                        weight[cell : cell + 1, :] * picked[group * width : (group + 1) * width, :]
                    )
            total = total.astype(BF16)
            for half in range(2):
                rows = pl.ds(pl.multiple_of((2 * span + half) * width, width), width)
                grid[rows, pl.ds(place, LANES)] += total[:, half * LANES : (half + 1) * LANES]
            return 0

        first = low // SPAN
        last = jnp.where(high > low, (high + SPAN - 1) // SPAN, first)
        lax.fori_loop(first, last, span_step, 0)
        return 0

    lax.fori_loop(0, count * SLOTS, job, 0)
    spectra = lax.dot_general(
        table[...], grid[...], (((1,), (1,)), ((), ())), preferred_element_type=F32
    )
    out[...] = spectra.astype(BF16)


def final_body(chunks, lat_rows, per_step, legendre, *rest):
    parts, (out, gathered, factor) = rest[: len(chunks)], rest[len(chunks) :]
    sources, waves, _ = parts[0].shape
    degrees = legendre.shape[2]

    @pl.when(pl.program_id(0) == 0)
    def _():
        degree = lax.broadcasted_iota(jnp.int32, factor.shape, 0).astype(F32)
        factor[...] = 1.0 / (1.0 + 4.0 * degree * (degree + 1.0) / (degrees * (degrees + 1)))
        lane = lax.broadcasted_iota(jnp.int32, (waves, LANES), 1)

        def gather(source, _):
            for row in range(lat_rows):
                total = None
                for part, (first, width) in zip(parts, chunks, strict=True):
                    groups = LANES // width
                    tile, group = row // groups, row % groups
                    values = part[source, :, tile * LANES : (tile + 1) * LANES].astype(F32)
                    shift = (first - group * width) % LANES
                    if shift:
                        values = pltpu.roll(values, shift, 1)
                    total = values if total is None else jnp.where(lane >= first, values, total)
                start = pl.multiple_of((source * lat_rows + row) * waves, 8)
                gathered[pl.ds(start, waves), :] = total
            return 0

        lax.fori_loop(0, sources, gather, 0)

    for step in range(per_step):
        wave = pl.program_id(0) * per_step + step
        column = gathered[pl.ds(wave, sources * lat_rows, stride=waves), :].astype(BF16)
        projected = lax.dot_general(
            legendre[step], column, (((0,), (0,)), ((), ())), preferred_element_type=F32
        )
        out[step] = projected * factor[...]


def whole(shape):
    return pl.BlockSpec(shape, lambda *_: (0,) * len(shape))


VMEM = pl.BlockSpec(memory_space=pltpu.VMEM)
SMEM = pl.BlockSpec(memory_space=pltpu.SMEM)
LIMIT = pltpu.CompilerParams(vmem_limit_bytes=56 * 2**20)


def gathering(fields, req_block, req_stencil, req_frac, req_count, legendre):
    lat_rows, lon_cols, channels = fields.shape
    waves, lat_total, degrees = legendre.shape
    count, bands = lax.axis_size("lon"), lax.axis_size("lat")
    cells = lat_rows * lon_cols
    blocks = cells // BLK
    lon_total = lon_cols * count
    sector_waves = waves * bands
    chunks = chunk_list(channels)
    me = lax.axis_index("lon")
    here = jnp.full((1,), me, jnp.int32)

    table = hartley_table(sector_waves * count, lon_total)
    table = lax.dynamic_slice_in_dim(table, me * sector_waves, sector_waves, axis=0)

    tile_rows = [blocks * BLK * width // LANES for _, width in chunks]
    tile_rows[0] += cells // LANES * 8
    packed = pl.pallas_call(
        functools.partial(pack_body, chunks, blocks),
        out_shape=[jax.ShapeDtypeStruct((rows, LANES), BF16) for rows in tile_rows],
        in_specs=[SMEM, VMEM, VMEM, VMEM, VMEM],
        out_specs=[VMEM] * len(chunks),
        scratch_shapes=[pltpu.VMEM((cells, channels), F32)],
        compiler_params=LIMIT,
    )(req_count[0, 0], fields.reshape(cells, channels), req_block[0, 0], req_stencil[0, 0], req_frac[0, 0])

    parts = []
    ends = params = None
    for number, (first, width) in enumerate(chunks):
        below, above = [packed[number]], [packed[number]]
        for away in range(1, count):
            below.append(lax.ppermute(below[-1], "lon", [(i, i + 1) for i in range(away - 1, count - 1)]))
            above.append(lax.ppermute(above[-1], "lon", [(i + 1, i) for i in range(count - away)]))
        tiles = below + above[1:]
        lead = number == 0
        out_shape = [jax.ShapeDtypeStruct((sector_waves, lat_rows * width), BF16)]
        out_specs = [VMEM]
        given = [here]
        if lead:
            out_shape += [
                jax.ShapeDtypeStruct((count, cells // LANES * 8, LANES), BF16),
                jax.ShapeDtypeStruct((count, SLOTS + 1), jnp.int32),
            ]
            out_specs += [VMEM, SMEM]
        else:
            given += [ends, params]
        results = pl.pallas_call(
            functools.partial(interp_body, count, width, blocks, lead),
            out_shape=out_shape,
            in_specs=[SMEM] + ([] if lead else [SMEM, VMEM]) + [VMEM] * (len(tiles) + 1),
            out_specs=out_specs,
            scratch_shapes=[
                pltpu.VMEM((count, BLK * width, blocks), BF16),
                pltpu.VMEM((lat_rows * width, lon_total), BF16),
            ],
            compiler_params=LIMIT,
            cost_estimate=pl.CostEstimate(flops=width * 10**7, bytes_accessed=10**6, transcendentals=0),
        )(*given, *tiles, table)
        if lead:
            fourier, params, ends = results
        else:
            (fourier,) = results
        fourier = fourier.reshape(bands, waves, lat_rows * width)
        parts.append(lax.all_to_all(fourier, "lat", split_axis=0, concat_axis=0, tiled=True))

    per_step = math.gcd(waves, 4)
    return pl.pallas_call(
        functools.partial(final_body, chunks, lat_rows, per_step),
        grid=(waves // per_step,),
        out_shape=jax.ShapeDtypeStruct((waves, degrees, channels), F32),
        in_specs=[pl.BlockSpec((per_step, lat_total, degrees), lambda i: (i, 0, 0))]
        + [whole(part.shape) for part in parts],
        out_specs=pl.BlockSpec((per_step, degrees, channels), lambda i: (i, 0, 0)),
        scratch_shapes=[
            pltpu.VMEM((lat_total * waves, channels), F32),
            pltpu.VMEM((degrees, channels), F32),
        ],
        compiler_params=LIMIT,
    )(legendre, *parts)


def padded(cells, sides, width):
    for axis, dim in sides:
        count = lax.axis_size(axis)
        head = lax.slice_in_dim(cells, 0, width, axis=dim)
        tail = lax.slice_in_dim(cells, cells.shape[dim] - width, cells.shape[dim], axis=dim)
        cells = jnp.concatenate(
            [
                lax.ppermute(tail, axis, [(i, (i + 1) % count) for i in range(count)]),
                cells,
                lax.ppermute(head, axis, [((i + 1) % count, i) for i in range(count)]),
            ],
            axis=dim,
        )
    return cells


def interpolate(own_tile, packed):
    cell_rows = packed[0][None, :] * BLK + packed[1:5]
    picked = jnp.take(own_tile, cell_rows.reshape(-1), axis=0).astype(F32)
    picked = picked.reshape(4, cell_rows.shape[1], own_tile.shape[1])
    frac_lat = (packed[5].astype(F32) + 0.5) / FRAC
    frac_lon = (packed[6].astype(F32) + 0.5) / FRAC
    weights = jnp.stack(
        [
            (1.0 - frac_lat) * (1.0 - frac_lon),
            frac_lat * (1.0 - frac_lon),
            (1.0 - frac_lat) * frac_lon,
            frac_lat * frac_lon,
        ]
    )
    return jnp.sum(weights[:, :, None] * picked, axis=0).astype(BF16)


def place_columns(values, counts, columns):
    slot_ends = jnp.cumsum(counts)
    starts = slot_ends - counts
    column = jnp.arange(columns, dtype=jnp.int32)
    slot_index = jnp.sum((slot_ends[None, :] <= column[:, None]).astype(jnp.int32), axis=1)
    onehot = slot_index[:, None] == jnp.arange(SLOTS, dtype=jnp.int32)[None, :]
    offset = column - jnp.sum(jnp.where(onehot, starts[None, :], 0), axis=1)
    flat_index = slot_index * values.shape[1] + offset
    return jnp.take(values.reshape(-1, values.shape[-1]), flat_index, axis=0)


def exchanging(fields, req_block, req_stencil, req_frac, req_count, legendre):
    lat_rows, lon_cols, channels = fields.shape
    count = lax.axis_size("lon")
    waves_total = legendre.shape[0] * count * lax.axis_size("lat")
    packed = jnp.concatenate(
        [req_block[0, 0][:, None, :], req_stencil[0, 0], req_frac[0, 0]], axis=1
    )
    counts = req_count[0, 0]
    widened = padded(fields, (("lon", 1),), lon_cols)
    slot_values = []
    for slot_index in range(SLOTS):
        owner_tile = widened[:, slot_index * lon_cols : (slot_index + 1) * lon_cols, :].reshape(
            -1, channels
        )
        slot_values.append(interpolate(owner_tile, packed[slot_index]))
    departed = place_columns(jnp.stack(slot_values), counts, lat_rows * lon_cols)
    departed = departed.reshape(lat_rows, lon_cols, channels)
    lon_total = lon_cols * count
    spectra = jnp.einsum(
        "kx,yxc->ykc",
        hartley_table(waves_total, lon_total),
        lax.all_to_all(departed, "lon", split_axis=0, concat_axis=1, tiled=True),
        preferred_element_type=F32,
    )
    fourier = lax.all_to_all(spectra.astype(BF16), "lon", split_axis=1, concat_axis=0, tiled=True)
    gathered = lax.all_to_all(fourier, "lat", split_axis=1, concat_axis=0, tiled=True)
    projected = jnp.einsum("kyn,ykc->knc", legendre, gathered, preferred_element_type=F32)
    degrees = legendre.shape[2]
    degree = jnp.arange(degrees, dtype=F32)
    factor = 1.0 / (1.0 + 4.0 * degree * (degree + 1.0) / (degrees * (degrees + 1)))
    return projected * factor[None, :, None]


def local(fields, req_block, req_stencil, req_frac, req_count, legendre):
    count = lax.axis_size("lon")
    lon_cols = fields.shape[1]
    sector_waves = legendre.shape[0] * lax.axis_size("lat")
    plan = gathering if count * lon_cols <= lon_cols + sector_waves else exchanging
    return plan(fields, req_block, req_stencil, req_frac, req_count, legendre)


def solution(mesh):
    return jax.shard_map(
        local,
        mesh=mesh,
        in_specs=(
            P("lat", "lon", None),
            P("lat", "lon", None, None),
            P("lat", "lon", None, None, None),
            P("lat", "lon", None, None, None),
            P("lat", "lon", None),
            P(("lon", "lat"), None, None),
        ),
        out_specs=P(("lon", "lat"), None, None),
        check_vma=False,
    )
```

```python
import functools
import math

import jax
import jax.numpy as jnp
from jax import lax
from jax.experimental import pallas as pl
from jax.experimental.pallas import tpu as pltpu
from jax.sharding import PartitionSpec as P

BLK = 16
FRAC = 16
SLOTS = 3
LANES = 128
SPAN = 2 * LANES
F32 = jnp.float32
BF16 = jnp.bfloat16


def hartley_table(waves, lon_total):
    wave_index = jnp.arange(waves, dtype=jnp.int32)
    lon_index = jnp.arange(lon_total, dtype=jnp.int32)
    phase_index = wave_index[:, None] * lon_index[None, :] % lon_total
    phase_angle = 2.0 * math.pi / lon_total * phase_index.astype(F32)
    return ((jnp.cos(phase_angle) + jnp.sin(phase_angle)) / math.sqrt(lon_total)).astype(BF16)


def chunk_list(channels):
    half = channels // 2
    return ((0, half), (half, half))


def pack_body(chunks, blocks, counts, fields, block, stencil, frac, *rest):
    outs, wide = rest[:-1], rest[-1]
    cells = blocks * BLK
    cap = block.shape[1]
    wide[...] = fields[...].astype(F32)
    lane = lax.broadcasted_iota(jnp.int32, (blocks, LANES), 1)
    for out, (first, width) in zip(outs, chunks, strict=True):
        groups = LANES // width
        planes = BLK // groups
        for plane in range(planes):
            total = None
            for group in range(groups):
                rows = wide[pl.ds(group * planes + plane, blocks, stride=BLK), :]
                shift = (group * width - first) % LANES
                if shift:
                    rows = pltpu.roll(rows, shift, 1)
                total = rows if total is None else jnp.where(lane >= group * width, rows, total)
            out[plane * blocks : (plane + 1) * blocks, :] = total.astype(BF16)
    starts = (0, counts[0], counts[0] + counts[1])
    column = lax.broadcasted_iota(jnp.int32, (8, cells), 1)
    row = lax.broadcasted_iota(jnp.int32, (8, cells), 0)
    slot = (column >= starts[1]).astype(jnp.int32) + (column >= starts[2]).astype(jnp.int32)
    placed = slot.astype(F32)
    for index in range(SLOTS):
        listed = jnp.concatenate(
            [
                block[index : index + 1, :].astype(F32),
                stencil[index].astype(F32),
                frac[index].astype(F32),
                jnp.zeros((1, cap), F32),
            ],
            axis=0,
        )
        listed = jnp.concatenate([listed, jnp.zeros((8, cells - cap), F32)], axis=1)
        if index:
            listed = pltpu.roll(listed, starts[index], 1)
        placed = jnp.where((slot == index) & (row < 7), listed, placed)
    base = outs[0].shape[0] - cells // LANES * 8
    for span in range(cells // SPAN):
        pair = jnp.concatenate(
            [
                placed[:, span * SPAN : span * SPAN + LANES],
                placed[:, span * SPAN + LANES : (span + 1) * SPAN],
            ],
            axis=0,
        )
        outs[0][base + span * 16 : base + (span + 1) * 16, :] = pair.astype(BF16)


def interp_body(count, width, blocks, lead, late, reach, here, *rest):
    tiles, rest = rest[: len(reach)], rest[len(reach) :]
    if not lead:
        (params, ends), rest = rest[:2], rest[2:]
    if late:
        (given, table), rest = rest[:2], rest[2:]
        (out, *rest), grid = rest[:-1], rest[-1]
    else:
        grid, *rest = rest
    if lead:
        params, ends, flipped = rest
    else:
        (flipped,) = rest
    me = here[0]
    far = count - 1
    groups = LANES // width
    planes = BLK // groups
    sign = 1 - 2 * lax.rem(me, 2)
    owners = [me + side * sign * away for away, side in reach]

    def present(number):
        return (owners[number] >= 0) & (owners[number] < count)

    def take(tile, owner):
        for plane in range(planes):
            rows = tile[plane * blocks : (plane + 1) * blocks, :]
            flipped[owner, plane * LANES : (plane + 1) * LANES, :] = rows.T

    if lead:
        for number, tile in enumerate(tiles):

            @pl.when(present(number))
            def _(number=number, tile=tile):
                params[owners[number]] = tile[planes * blocks :, :]

        for tile in range(count):
            ends[tile, 0] = 0

            @pl.when(late | (jnp.abs(me - tile) < far))
            def _(tile=tile):
                rows = params[tile].astype(F32)
                which = lax.broadcasted_iota(jnp.int32, rows.shape, 0) % 8 == 7
                for index in range(SLOTS):
                    listed = jnp.where(which & (rows <= index), 1.0, 0.0)
                    ends[tile, index + 1] = jnp.sum(listed).astype(jnp.int32)

    if late:
        grid[...] = given[...]
    else:
        grid[...] = jnp.zeros_like(grid)

    block_row = lax.broadcasted_iota(jnp.int32, (blocks, SPAN), 0).astype(F32)
    cell_row = lax.broadcasted_iota(jnp.int32, (BLK, SPAN), 0).astype(F32)

    def wanted(owner, index):
        target = lax.rem(owner - index + 1 + count, count)
        if not lead:
            return jnp.bool_(True)
        distant = jnp.maximum(jnp.abs(target - me), jnp.abs(owner - me)) == far
        return distant if late else jnp.logical_not(distant)

    def job(owner, index):
        target = lax.rem(owner - index + 1 + count, count)
        low = ends[target, index]
        high = ends[target, index + 1]
        place = pl.multiple_of(target * LANES, LANES)
        first = low // SPAN
        last = jnp.where(high > low, (high + SPAN - 1) // SPAN, first)

        def span_step(span, valid):
            both = params[target, pl.ds(pl.multiple_of(span * 16, 16), 16), :].astype(F32)

            def line(i):
                return jnp.concatenate([both[i : i + 1, :], both[8 + i : 9 + i, :]], axis=1)

            mine = line(7) == jnp.where(valid, index, -1).astype(F32)
            key = jnp.where(mine, line(0), -1.0)
            onehot = jnp.where(block_row == key, 1.0, 0.0).astype(BF16)
            f_lat = (line(5) + 0.5) / FRAC
            f_lon = (line(6) + 0.5) / FRAC
            corners = (
                (1.0 - f_lat) * (1.0 - f_lon),
                f_lat * (1.0 - f_lon),
                (1.0 - f_lat) * f_lon,
                f_lat * f_lon,
            )
            weight = jnp.zeros((BLK, SPAN), F32)
            for corner in range(4):
                weight += jnp.where(cell_row == line(1 + corner), corners[corner], 0.0)
            picked = jnp.dot(flipped[owner], onehot, preferred_element_type=F32)
            total = jnp.zeros((width, SPAN), F32)
            for cell in range(BLK):
                start = cell % planes * LANES + cell // planes * width
                total += weight[cell : cell + 1, :] * picked[start : start + width, :]
            return total.astype(BF16)

        def add(span, total):
            for half in range(2):
                rows = pl.ds(pl.multiple_of((2 * span + half) * width, width), width)
                grid[rows, pl.ds(place, LANES)] += total[:, half * LANES : (half + 1) * LANES]

        def pair_step(pair, _):
            one = first + 2 * pair
            two = jnp.minimum(one + 1, last - 1)
            total_one = span_step(one, True)
            total_two = span_step(two, one + 1 < last)
            add(one, total_one)
            add(two, total_two)
            return 0

        lax.fori_loop(0, (last - first + 1) // 2, pair_step, 0)

    for number, tile in enumerate(tiles):
        owner = owners[number]
        needed = present(number)
        if lead and late:
            asked = [wanted(owner, index) for index in range(SLOTS)]
            needed = needed & functools.reduce(jnp.logical_or, asked)

        @pl.when(needed)
        def _(tile=tile, owner=owner):
            take(tile, owner)

            def each(index, _):
                @pl.when(wanted(owner, index))
                def _():
                    job(owner, index)

                return 0

            lax.fori_loop(0, SLOTS, each, 0)

    if late:
        out[...] = lax.dot_general(
            table[...], grid[...], (((1,), (1,)), ((), ())), preferred_element_type=F32
        ).astype(BF16)


def collect_body(chunks, lat_rows, *rest):
    parts, gathered = rest[:-1], rest[-1]
    bands, waves, _ = parts[0].shape
    lane = lax.broadcasted_iota(jnp.int32, (waves, LANES), 1)

    def collect(source, _):
        for row in range(lat_rows):
            total = None
            for part, (first, width) in zip(parts, chunks, strict=True):
                groups = LANES // width
                tile, group = row // groups, row % groups
                values = part[source, :, tile * LANES : (tile + 1) * LANES].astype(F32)
                turn = (first - group * width) % LANES
                if turn:
                    values = pltpu.roll(values, turn, 1)
                total = values if total is None else jnp.where(lane >= first, values, total)
            start = pl.multiple_of((source * lat_rows + row) * waves, 8)
            gathered[pl.ds(start, waves), :] = total
        return 0

    lax.fori_loop(0, bands, collect, 0)


def final_body(last, lat_rows, per_step, legendre, early, part, out, gathered, factor, staged, done):
    waves, lat_total, degrees = legendre.shape
    bands = part.shape[0]
    first, width = last
    degree = lax.broadcasted_iota(jnp.int32, factor.shape, 0).astype(F32)
    factor[...] = 1.0 / (1.0 + 4.0 * degree * (degree + 1.0) / (degrees * (degrees + 1)))
    lane = lax.broadcasted_iota(jnp.int32, (waves, LANES), 1)
    groups = LANES // width

    def collect(source, _):
        for row in range(lat_rows):
            tile, group = row // groups, row % groups
            values = part[source, :, tile * LANES : (tile + 1) * LANES].astype(F32)
            turn = (first - group * width) % LANES
            if turn:
                values = pltpu.roll(values, turn, 1)
            rows = pl.ds(pl.multiple_of((source * lat_rows + row) * waves, 8), waves)
            gathered[rows, :] = jnp.where(lane >= first, values, early[rows, :])
        return 0

    lax.fori_loop(0, bands, collect, 0)

    def step(number, _):
        for inner in range(per_step):
            wave = number * per_step + inner
            column = gathered[pl.ds(wave, lat_total, stride=waves), :].astype(BF16)
            projected = lax.dot_general(
                legendre[wave], column, (((0,), (0,)), ((), ())), preferred_element_type=F32
            )
            staged[wave] = projected * factor[...]
        rows = pl.ds(number * per_step, per_step)
        pltpu.make_async_copy(staged.at[rows], out.at[rows], done).start()
        return 0

    lax.fori_loop(0, waves // per_step, step, 0)
    pltpu.make_async_copy(staged, out, done).wait()


VMEM = pl.BlockSpec(memory_space=pltpu.VMEM)
SMEM = pl.BlockSpec(memory_space=pltpu.SMEM)
ANY = pl.BlockSpec(memory_space=pl.ANY)


def limit(mib):
    return pltpu.CompilerParams(vmem_limit_bytes=mib * 2**20)


def cost(flops):
    return pl.CostEstimate(flops=flops, bytes_accessed=10**6, transcendentals=0)


def gathering(fields, req_block, req_stencil, req_frac, req_count, legendre):
    lat_rows, lon_cols, channels = fields.shape
    waves, lat_total, degrees = legendre.shape
    count, bands = lax.axis_size("lon"), lax.axis_size("lat")
    cells = lat_rows * lon_cols
    blocks = cells // BLK
    lon_total = lon_cols * count
    sector_waves = waves * bands
    chunks = chunk_list(channels)
    me = lax.axis_index("lon")
    here = jnp.full((1,), me, jnp.int32)

    table = hartley_table(sector_waves * count, lon_total)
    table = lax.dynamic_slice_in_dim(table, me * sector_waves, sector_waves, axis=0)

    tile_rows = [blocks * BLK * width // LANES for _, width in chunks]
    tile_rows[0] += cells // LANES * 8
    packed = pl.pallas_call(
        functools.partial(pack_body, chunks, blocks),
        out_shape=[jax.ShapeDtypeStruct((rows, LANES), BF16) for rows in tile_rows],
        in_specs=[SMEM, VMEM, VMEM, VMEM, VMEM],
        out_specs=[VMEM] * len(tile_rows),
        scratch_shapes=[pltpu.VMEM((cells, channels), F32)],
        compiler_params=limit(16),
        name="pack",
    )(req_count[0, 0], fields.reshape(cells, channels), req_block[0, 0], req_stencil[0, 0], req_frac[0, 0])

    def links(parity, away):
        up = [(i, i + 1) for i in range(parity, count - 1, 2) if i - away + 1 >= 0]
        down = [(i + 1, i) for i in range(parity, count - 1, 2) if i + away < count]
        return up + down

    held = [[(packed[number], 0, 1)] for number in range(len(chunks))]
    edge = [(tile, tile) for tile in packed]
    for away in range(1, count):
        for number in range(len(chunks)):
            even, odd = edge[number]
            both = []
            for parity, tile, side in ((0, odd, 1), (1, even, -1)):
                pairs = links(parity, away)
                both.append(lax.ppermute(tile, "lon", pairs) if pairs else None)
                if pairs:
                    held[number].append((both[-1], away, side))
            edge[number] = tuple(both)

    parts = []
    params = ends = None
    for number, (first, width) in enumerate(chunks):
        lead = number == 0
        soon = [one for one in held[number] if one[1] < count - 1]
        last = held[number] if lead else [one for one in held[number] if one[1] == count - 1]
        flipped = pltpu.VMEM((count, BLK * width, blocks), BF16)
        grid = jax.ShapeDtypeStruct((lat_rows * width, lon_total), BF16)
        listed = [
            jax.ShapeDtypeStruct((count, cells // LANES * 8, LANES), BF16),
            jax.ShapeDtypeStruct((count, SLOTS + 1), jnp.int32),
        ]
        given = [] if lead else [params, ends]
        given_specs = [] if lead else [VMEM, SMEM]
        kept = [pltpu.VMEM(listed[0].shape, BF16), pltpu.SMEM(listed[1].shape, jnp.int32)]
        grid = pl.pallas_call(
            functools.partial(interp_body, count, width, blocks, lead, False, [one[1:] for one in soon]),
            out_shape=grid,
            in_specs=[SMEM] + [VMEM] * len(soon) + given_specs,
            out_specs=VMEM,
            scratch_shapes=(kept if lead else []) + [flipped],
            compiler_params=limit(24),
            cost_estimate=cost(width * 10**8),
            name="early",
        )(here, *[one[0] for one in soon], *given)
        fourier, *found = pl.pallas_call(
            functools.partial(interp_body, count, width, blocks, lead, True, [one[1:] for one in last]),
            out_shape=[jax.ShapeDtypeStruct((sector_waves, lat_rows * width), BF16)]
            + (listed if lead else []),
            in_specs=[SMEM] + [VMEM] * len(last) + given_specs + [VMEM, VMEM],
            out_specs=[VMEM] + ([VMEM, SMEM] if lead else []),
            scratch_shapes=[flipped, pltpu.VMEM(grid.shape, BF16)],
            compiler_params=limit(24),
            cost_estimate=cost(width * 5 * 10**7),
            name="late",
        )(here, *[one[0] for one in last], *given, grid, table)
        if lead:
            params, ends = found
        fourier = fourier.reshape(bands, waves, lat_rows * width)
        parts.append(lax.all_to_all(fourier, "lat", split_axis=0, concat_axis=0, tiled=True))

    gathered = jax.ShapeDtypeStruct((lat_total * waves, channels), F32)
    early = pl.pallas_call(
        functools.partial(collect_body, chunks[:-1], lat_rows),
        out_shape=gathered,
        in_specs=[VMEM] * (len(chunks) - 1),
        out_specs=VMEM,
        compiler_params=limit(16),
        cost_estimate=cost(10**9),
        name="collect",
    )(*parts[:-1])
    per_step = math.gcd(waves, 8)
    return pl.pallas_call(
        functools.partial(final_body, chunks[-1], lat_rows, per_step),
        out_shape=jax.ShapeDtypeStruct((waves, degrees, channels), F32),
        in_specs=[VMEM] * 3,
        out_specs=ANY,
        scratch_shapes=[
            pltpu.VMEM(gathered.shape, F32),
            pltpu.VMEM((degrees, channels), F32),
            pltpu.VMEM((waves, degrees, channels), F32),
            pltpu.SemaphoreType.DMA,
        ],
        compiler_params=limit(28),
        name="final",
    )(legendre, early, parts[-1])


def padded(cells, sides, width):
    for axis, dim in sides:
        count = lax.axis_size(axis)
        head = lax.slice_in_dim(cells, 0, width, axis=dim)
        tail = lax.slice_in_dim(cells, cells.shape[dim] - width, cells.shape[dim], axis=dim)
        cells = jnp.concatenate(
            [
                lax.ppermute(tail, axis, [(i, (i + 1) % count) for i in range(count)]),
                cells,
                lax.ppermute(head, axis, [((i + 1) % count, i) for i in range(count)]),
            ],
            axis=dim,
        )
    return cells


def interpolate(own_tile, packed):
    cell_rows = packed[0][None, :] * BLK + packed[1:5]
    picked = jnp.take(own_tile, cell_rows.reshape(-1), axis=0).astype(F32)
    picked = picked.reshape(4, cell_rows.shape[1], own_tile.shape[1])
    frac_lat = (packed[5].astype(F32) + 0.5) / FRAC
    frac_lon = (packed[6].astype(F32) + 0.5) / FRAC
    weights = jnp.stack(
        [
            (1.0 - frac_lat) * (1.0 - frac_lon),
            frac_lat * (1.0 - frac_lon),
            (1.0 - frac_lat) * frac_lon,
            frac_lat * frac_lon,
        ]
    )
    return jnp.sum(weights[:, :, None] * picked, axis=0).astype(BF16)


def place_columns(values, counts, columns):
    slot_ends = jnp.cumsum(counts)
    starts = slot_ends - counts
    column = jnp.arange(columns, dtype=jnp.int32)
    slot_index = jnp.sum((slot_ends[None, :] <= column[:, None]).astype(jnp.int32), axis=1)
    onehot = slot_index[:, None] == jnp.arange(SLOTS, dtype=jnp.int32)[None, :]
    offset = column - jnp.sum(jnp.where(onehot, starts[None, :], 0), axis=1)
    flat_index = slot_index * values.shape[1] + offset
    return jnp.take(values.reshape(-1, values.shape[-1]), flat_index, axis=0)


def exchanging(fields, req_block, req_stencil, req_frac, req_count, legendre):
    lat_rows, lon_cols, channels = fields.shape
    count = lax.axis_size("lon")
    waves_total = legendre.shape[0] * count * lax.axis_size("lat")
    packed = jnp.concatenate(
        [req_block[0, 0][:, None, :], req_stencil[0, 0], req_frac[0, 0]], axis=1
    )
    counts = req_count[0, 0]
    widened = padded(fields, (("lon", 1),), lon_cols)
    slot_values = []
    for slot_index in range(SLOTS):
        owner_tile = widened[:, slot_index * lon_cols : (slot_index + 1) * lon_cols, :].reshape(
            -1, channels
        )
        slot_values.append(interpolate(owner_tile, packed[slot_index]))
    departed = place_columns(jnp.stack(slot_values), counts, lat_rows * lon_cols)
    departed = departed.reshape(lat_rows, lon_cols, channels)
    lon_total = lon_cols * count
    spectra = jnp.einsum(
        "kx,yxc->ykc",
        hartley_table(waves_total, lon_total),
        lax.all_to_all(departed, "lon", split_axis=0, concat_axis=1, tiled=True),
        preferred_element_type=F32,
    )
    fourier = lax.all_to_all(spectra.astype(BF16), "lon", split_axis=1, concat_axis=0, tiled=True)
    gathered = lax.all_to_all(fourier, "lat", split_axis=1, concat_axis=0, tiled=True)
    projected = jnp.einsum("kyn,ykc->knc", legendre, gathered, preferred_element_type=F32)
    degrees = legendre.shape[2]
    degree = jnp.arange(degrees, dtype=F32)
    factor = 1.0 / (1.0 + 4.0 * degree * (degree + 1.0) / (degrees * (degrees + 1)))
    return projected * factor[None, :, None]


def local(fields, req_block, req_stencil, req_frac, req_count, legendre):
    count = lax.axis_size("lon")
    lon_cols = fields.shape[1]
    sector_waves = legendre.shape[0] * lax.axis_size("lat")
    plan = gathering if count * lon_cols <= lon_cols + sector_waves else exchanging
    return plan(fields, req_block, req_stencil, req_frac, req_count, legendre)


def solution(mesh):
    return jax.shard_map(
        local,
        mesh=mesh,
        in_specs=(
            P("lat", "lon", None),
            P("lat", "lon", None, None),
            P("lat", "lon", None, None, None),
            P("lat", "lon", None, None, None),
            P("lat", "lon", None),
            P(("lon", "lat"), None, None),
        ),
        out_specs=P(("lon", "lat"), None, None),
        check_vma=False,
    )
```

```python
import functools
import math

import jax
import jax.numpy as jnp
import numpy as np
from jax import lax
from jax.experimental import pallas as pl
from jax.experimental.pallas import tpu as pltpu
from jax.sharding import PartitionSpec as P

BLK = 16
FRAC = 16
SLOTS = 3
LANES = 128
SPAN = 2 * LANES
UNROLL = 4
F32 = jnp.float32
BF16 = jnp.bfloat16


def hartley_table(waves, lon_total):
    wave_index = jnp.arange(waves, dtype=jnp.int32)
    lon_index = jnp.arange(lon_total, dtype=jnp.int32)
    phase_index = wave_index[:, None] * lon_index[None, :] % lon_total
    phase_angle = 2.0 * math.pi / lon_total * phase_index.astype(F32)
    return ((jnp.cos(phase_angle) + jnp.sin(phase_angle)) / math.sqrt(lon_total)).astype(BF16)


def hartley_constant(waves, lon_total):
    phase_index = np.arange(waves)[:, None] * np.arange(lon_total)[None, :] % lon_total
    phase_angle = np.float32(2.0 * math.pi / lon_total) * phase_index.astype(np.float32)
    table = (np.cos(phase_angle) + np.sin(phase_angle)) / np.float32(math.sqrt(lon_total))
    return jnp.asarray(table.astype(BF16))


def chunk_list(channels):
    half = channels // 2
    return ((0, half), (half, half))


def pack_body(chunks, blocks, counts, fields, block, stencil, frac, *rest):
    outs, (wide, *held, done) = rest[: len(chunks)], rest[len(chunks) :]
    copies = [
        pltpu.make_async_copy(given, kept, done.at[number])
        for number, (given, kept) in enumerate(zip((counts, fields, block, stencil, frac), held, strict=True))
    ]
    for copy in copies:
        copy.start()
    for copy in copies:
        copy.wait()
    counts, fields, block, stencil, frac = held
    cells = blocks * BLK
    cap = block.shape[1]
    wide[...] = fields[...].astype(F32)
    lane = lax.broadcasted_iota(jnp.int32, (blocks, LANES), 1)
    for out, (first, width) in zip(outs, chunks, strict=True):
        groups = LANES // width
        planes = BLK // groups
        for plane in range(planes):
            total = None
            for group in range(groups):
                rows = wide[pl.ds(group * planes + plane, blocks, stride=BLK), :]
                shift = (group * width - first) % LANES
                if shift:
                    rows = pltpu.roll(rows, shift, 1)
                total = rows if total is None else jnp.where(lane >= group * width, rows, total)
            out[plane * blocks : (plane + 1) * blocks, :] = total.astype(BF16)
    starts = (0, counts[0], counts[0] + counts[1])
    column = lax.broadcasted_iota(jnp.int32, (8, cells), 1)
    row = lax.broadcasted_iota(jnp.int32, (8, cells), 0)
    slot = (column >= starts[1]).astype(jnp.int32) + (column >= starts[2]).astype(jnp.int32)
    placed = slot.astype(F32)
    for index in range(SLOTS):
        listed = jnp.concatenate(
            [
                block[index : index + 1, :].astype(F32),
                stencil[index].astype(F32),
                frac[index].astype(F32),
                jnp.zeros((1, cap), F32),
            ],
            axis=0,
        )
        listed = jnp.concatenate([listed, jnp.zeros((8, cells - cap), F32)], axis=1)
        if index:
            listed = pltpu.roll(listed, starts[index], 1)
        placed = jnp.where((slot == index) & (row < 7), listed, placed)
    base = outs[0].shape[0] - cells // LANES * 8
    for span in range(cells // SPAN):
        pair = jnp.concatenate(
            [
                placed[:, span * SPAN : span * SPAN + LANES],
                placed[:, span * SPAN + LANES : (span + 1) * SPAN],
            ],
            axis=0,
        )
        outs[0][base + span * 16 : base + (span + 1) * 16, :] = pair.astype(BF16)


def interp_body(count, bands, width, blocks, lead, late, far, reach, here, *rest):
    tiles, rest = rest[: len(reach)], rest[len(reach) :]
    if not lead:
        (params, ends), rest = rest[:2], rest[2:]
    if late:
        (given, table), rest = rest[:2], rest[2:]
        outs, rest, (grid, spectra) = rest[:bands], rest[bands:-2], rest[-2:]
    else:
        grid, *rest = rest
    if lead:
        params, ends, flipped, work = rest
    else:
        flipped, work = rest
    me = here[0]
    groups = LANES // width
    planes = BLK // groups
    owners = [jnp.bitwise_xor(me, step) for step, _ in reach]

    def distant(other):
        step = jnp.bitwise_xor(me, other)
        return functools.reduce(jnp.logical_or, [step == one for one in far], jnp.bool_(False))

    def present(number):
        return (jnp.abs(me - owners[number]) <= count // 2) == reach[number][1]

    def take(tile, owner):
        for plane in range(planes):
            rows = tile[plane * blocks : (plane + 1) * blocks, :]
            flipped[owner, plane * LANES : (plane + 1) * LANES, :] = rows.T

    if lead:
        for number, tile in enumerate(tiles):

            @pl.when(present(number))
            def _(number=number, tile=tile):
                params[owners[number]] = tile[planes * blocks :, :]

        for tile in range(count):
            ends[tile, 0] = 0

            @pl.when(late | jnp.logical_not(distant(tile)))
            def _(tile=tile):
                rows = params[tile].astype(F32)
                which = lax.broadcasted_iota(jnp.int32, rows.shape, 0) % 8 == 7
                for index in range(SLOTS):
                    listed = jnp.where(which & (rows <= index), 1.0, 0.0)
                    ends[tile, index + 1] = jnp.sum(listed).astype(jnp.int32)

    if late:
        grid[...] = given[...]
    else:
        grid[...] = jnp.zeros_like(grid)

    block_row = lax.broadcasted_iota(jnp.int32, (blocks, SPAN), 0).astype(F32)
    cell_row = lax.broadcasted_iota(jnp.int32, (BLK, SPAN), 0).astype(F32)

    def wanted(owner, index):
        target = lax.rem(owner - index + 1 + count, count)
        if not lead:
            return jnp.bool_(True)
        either = distant(target) | distant(owner)
        return either if late else jnp.logical_not(either)

    spans = blocks * BLK // SPAN
    entries = jnp.int32(0)
    for number, tile in enumerate(tiles):
        owner = owners[number]
        asked = [present(number) & wanted(owner, index) for index in range(SLOTS)]

        @pl.when(functools.reduce(jnp.logical_or, asked))
        def _(tile=tile, owner=owner):
            take(tile, owner)

        for index in range(SLOTS):
            target = lax.rem(owner - index + 1 + count, count)
            target = jnp.where(asked[index], target, 0)
            low = ends[target, index]
            high = ends[target, index + 1]
            first = low // SPAN
            extra = (high + SPAN - 1) // SPAN - first
            extra = jnp.where(asked[index] & (high > low), extra, 0)
            code = ((owner * count + target) * SLOTS + index) * spans + first

            def enter(span, _, code=code, entries=entries):
                work[entries + span] = code + span
                return 0

            lax.fori_loop(0, extra, enter, 0)
            entries = entries + extra

    def entry_step(entry):
        code = work[jnp.minimum(entry, entries - 1)]
        span = lax.rem(code, spans)
        code = code // spans
        index = jnp.where(entry < entries, lax.rem(code, SLOTS), -1)
        code = code // SLOTS
        target, owner = lax.rem(code, count), code // count
        both = params[target, pl.ds(pl.multiple_of(span * 16, 16), 16), :].astype(F32)

        def line(i):
            return jnp.concatenate([both[i : i + 1, :], both[8 + i : 9 + i, :]], axis=1)

        key = jnp.where(line(7) == index.astype(F32), line(0), -1.0)
        onehot = jnp.where(block_row == key, 1.0, 0.0).astype(BF16)
        f_lat = (line(5) + 0.5) / FRAC
        f_lon = (line(6) + 0.5) / FRAC
        corners = (
            (1.0 - f_lat) * (1.0 - f_lon),
            f_lat * (1.0 - f_lon),
            (1.0 - f_lat) * f_lon,
            f_lat * f_lon,
        )
        weight = jnp.zeros((BLK, SPAN), F32)
        for corner in range(4):
            weight += jnp.where(cell_row == line(1 + corner), corners[corner], 0.0)
        total = jnp.zeros((width, SPAN), F32)
        for plane in range(planes):
            picked = jnp.dot(
                flipped[owner, plane * LANES : (plane + 1) * LANES, :],
                onehot,
                preferred_element_type=F32,
            )
            for group in range(groups):
                cell = group * planes + plane
                total += (
                    weight[cell : cell + 1, :] * picked[group * width : (group + 1) * width, :]
                )
        return span, pl.multiple_of(target * LANES, LANES), total.astype(BF16)

    def step(number, _):
        found = [entry_step(number * UNROLL + inner) for inner in range(UNROLL)]
        for span, place, total in found:
            for half in range(2):
                rows = pl.ds(pl.multiple_of((2 * span + half) * width, width), width)
                grid[rows, pl.ds(place, LANES)] += total[:, half * LANES : (half + 1) * LANES]
        return 0

    lax.fori_loop(0, (entries + UNROLL - 1) // UNROLL, step, 0)

    if late:
        spectra[...] = lax.dot_general(
            table[...], grid[...], (((1,), (1,)), ((), ())), preferred_element_type=F32
        ).astype(BF16)
        waves = outs[0].shape[0]
        for shift, out in enumerate(outs):
            start = pl.multiple_of(jnp.bitwise_xor(here[1], shift) * waves, 16)
            out[...] = spectra[pl.ds(start, waves), :]


def spread_rows(piece, row, first, width):
    groups = LANES // width
    tile, group = row // groups, row % groups
    values = piece[:, tile * LANES : (tile + 1) * LANES].astype(F32)
    turn = (first - group * width) % LANES
    return pltpu.roll(values, turn, 1) if turn else values


def collect_body(chunks, bands, lat_rows, here, *rest):
    pieces, gathered = rest[:-1], rest[-1]
    waves = pieces[0].shape[0]
    lane = lax.broadcasted_iota(jnp.int32, (waves, LANES), 1)
    for shift in range(bands):
        source = jnp.bitwise_xor(here[1], shift)
        for row in range(lat_rows):
            total = None
            for part, (first, width) in enumerate(chunks):
                values = spread_rows(pieces[part * bands + shift], row, first, width)
                total = values if total is None else jnp.where(lane >= first, values, total)
            start = pl.multiple_of((source * lat_rows + row) * waves, 8)
            gathered[pl.ds(start, waves), :] = total


def final_body(last, bands, lat_rows, per_step, here, legendre, early, *rest):
    pieces, (out, gathered, factor, staged, done) = rest[:bands], rest[bands:]
    waves, lat_total, degrees = legendre.shape
    first, width = last
    degree = lax.broadcasted_iota(jnp.int32, factor.shape, 0).astype(F32)
    factor[...] = 1.0 / (1.0 + 4.0 * degree * (degree + 1.0) / (degrees * (degrees + 1)))
    lane = lax.broadcasted_iota(jnp.int32, (waves, LANES), 1)
    for shift in range(bands):
        source = jnp.bitwise_xor(here[1], shift)
        for row in range(lat_rows):
            values = spread_rows(pieces[shift], row, first, width)
            rows = pl.ds(pl.multiple_of((source * lat_rows + row) * waves, 8), waves)
            gathered[rows, :] = jnp.where(lane >= first, values, early[rows, :])

    def step(number, _):
        for inner in range(per_step):
            wave = number * per_step + inner
            column = gathered[pl.ds(wave, lat_total, stride=waves), :].astype(BF16)
            projected = lax.dot_general(
                legendre[wave], column, (((0,), (0,)), ((), ())), preferred_element_type=F32
            )
            staged[wave] = projected * factor[...]
        rows = pl.ds(number * per_step, per_step)
        pltpu.make_async_copy(staged.at[rows], out.at[rows], done).start()
        return 0

    lax.fori_loop(0, waves // per_step, step, 0)
    pltpu.make_async_copy(staged, out, done).wait()


VMEM = pl.BlockSpec(memory_space=pltpu.VMEM)
SMEM = pl.BlockSpec(memory_space=pltpu.SMEM)
ANY = pl.BlockSpec(memory_space=pl.ANY)


def limit(mib):
    return pltpu.CompilerParams(vmem_limit_bytes=mib * 2**20)


def cost(flops):
    return pl.CostEstimate(flops=flops, bytes_accessed=10**6, transcendentals=0)


def gathering(fields, req_block, req_stencil, req_frac, req_count, legendre):
    lat_rows, lon_cols, channels = fields.shape
    waves, lat_total, degrees = legendre.shape
    count, bands = lax.axis_size("lon"), lax.axis_size("lat")
    cells = lat_rows * lon_cols
    blocks = cells // BLK
    lon_total = lon_cols * count
    sector_waves = waves * bands
    chunks = chunk_list(channels)
    me = lax.axis_index("lon")
    here = jnp.stack([me, lax.axis_index("lat")]).astype(jnp.int32)

    table = hartley_constant(sector_waves * count, lon_total)
    table = lax.dynamic_slice_in_dim(table, me * sector_waves, sector_waves, axis=0)

    tile_rows = [blocks * BLK * width // LANES for _, width in chunks]
    tile_rows[0] += cells // LANES * 8
    packed = pl.pallas_call(
        functools.partial(pack_body, chunks, blocks),
        out_shape=[jax.ShapeDtypeStruct((rows, LANES), BF16) for rows in tile_rows],
        in_specs=[pl.BlockSpec(memory_space=pltpu.HBM)] * 5,
        out_specs=[VMEM] * len(tile_rows),
        scratch_shapes=[
            pltpu.VMEM((cells, channels), F32),
            pltpu.SMEM(req_count.shape[2:], jnp.int32),
            pltpu.VMEM((cells, channels), BF16),
            pltpu.VMEM(req_block.shape[2:], jnp.int32),
            pltpu.VMEM(req_stencil.shape[2:], jnp.int32),
            pltpu.VMEM(req_frac.shape[2:], jnp.int32),
            pltpu.SemaphoreType.DMA((5,)),
        ],
        compiler_params=limit(48),
        name="pack",
    )(req_count[0, 0], fields.reshape(cells, channels), req_block[0, 0], req_stencil[0, 0], req_frac[0, 0])

    near = [(i, i ^ step) for step in range(count) for i in range(count) if abs(i - (i ^ step)) <= count // 2]

    def after(tile, others):
        return lax.optimization_barrier((tile, *others))[0] if others else tile

    def exchange(tile, step, others=()):
        return lax.ppermute(after(tile, others), "lon", [pair for pair in near if pair[0] ^ pair[1] == step])

    def relay(tile, step):
        pairs = [(i ^ 1, i) for i in range(count) if (i, i ^ step) not in near]
        return lax.ppermute(tile, "lon", pairs)

    far = [step for step in range(count) if any((i, i ^ step) not in near for i in range(count))]
    parts = []
    params = ends = None
    ahead = moved = ()
    for number, (first, width) in enumerate(chunks):
        lead = number == 0
        tile = packed[number]
        near_tiles = {step: exchange(tile, step, ahead) for step in range(1, count) if step not in far}
        ahead = tuple(near_tiles.values())
        far_tiles = [(exchange(tile, step, ahead), step, True) for step in far]
        passed = [relay(near_tiles[step ^ 1], step) for step in far]
        far_tiles += [(got, step, False) for got, step in zip(passed, far, strict=True)]
        soon = [(tile, 0, True)] + [(got, step, True) for step, got in near_tiles.items()]
        last = soon + far_tiles if lead else far_tiles
        scratch = [
            pltpu.VMEM((count, BLK * width, blocks), BF16),
            pltpu.SMEM((count * SLOTS * (cells // SPAN + 1),), jnp.int32),
        ]
        grid = jax.ShapeDtypeStruct((lat_rows * width, lon_total), BF16)
        listed = [
            jax.ShapeDtypeStruct((count, cells // LANES * 8, LANES), BF16),
            jax.ShapeDtypeStruct((count, SLOTS + 1), jnp.int32),
        ]
        given = [] if lead else [params, ends]
        given_specs = [] if lead else [VMEM, SMEM]
        kept = [pltpu.VMEM(listed[0].shape, BF16), pltpu.SMEM(listed[1].shape, jnp.int32)]
        grid = pl.pallas_call(
            functools.partial(interp_body, count, bands, width, blocks, lead, False, far, [one[1:] for one in soon]),
            out_shape=grid,
            in_specs=[SMEM] + [VMEM] * len(soon) + given_specs,
            out_specs=VMEM,
            scratch_shapes=(kept if lead else []) + scratch,
            compiler_params=limit(24),
            cost_estimate=cost(width * 10**9),
            name="early",
        )(here, *[one[0] for one in soon], *given)
        ahead = (grid, *[got for got, _, _ in far_tiles])
        grid = after(grid, moved)
        results = pl.pallas_call(
            functools.partial(interp_body, count, bands, width, blocks, lead, True, far, [one[1:] for one in last]),
            out_shape=[jax.ShapeDtypeStruct((waves, lat_rows * width), BF16)] * bands
            + (listed if lead else []),
            in_specs=[SMEM] + [VMEM] * len(last) + given_specs + [VMEM, VMEM],
            out_specs=[VMEM] * bands + ([VMEM, SMEM] if lead else []),
            scratch_shapes=scratch
            + [
                pltpu.VMEM(grid.shape, BF16),
                pltpu.VMEM((sector_waves, lat_rows * width), BF16),
            ],
            compiler_params=limit(24),
            cost_estimate=cost(width * 5 * 10**7),
            name="late",
        )(here, *[one[0] for one in last], *given, grid, table)
        if lead:
            params, ends = results[bands:]
        pieces = [results[0]]
        for shift in range(1, bands):
            pieces.append(lax.ppermute(results[shift], "lat", [(i, i ^ shift) for i in range(bands)]))
        parts.append(pieces)
        moved = pieces[2:6]

    gathered = jax.ShapeDtypeStruct((lat_total * waves, channels), F32)
    early = [piece for pieces in parts[:-1] for piece in pieces]
    early = pl.pallas_call(
        functools.partial(collect_body, chunks[:-1], bands, lat_rows),
        out_shape=gathered,
        in_specs=[SMEM] + [VMEM] * len(early),
        out_specs=VMEM,
        compiler_params=limit(16),
        cost_estimate=cost(10**9),
        name="collect",
    )(here, *early)
    per_step = math.gcd(waves, 8)
    return pl.pallas_call(
        functools.partial(final_body, chunks[-1], bands, lat_rows, per_step),
        out_shape=jax.ShapeDtypeStruct((waves, degrees, channels), F32),
        in_specs=[SMEM] + [VMEM] * (bands + 2),
        out_specs=ANY,
        scratch_shapes=[
            pltpu.VMEM(gathered.shape, F32),
            pltpu.VMEM((degrees, channels), F32),
            pltpu.VMEM((waves, degrees, channels), F32),
            pltpu.SemaphoreType.DMA,
        ],
        compiler_params=limit(28),
        name="final",
    )(here, legendre, early, *parts[-1])


def padded(cells, sides, width):
    for axis, dim in sides:
        count = lax.axis_size(axis)
        head = lax.slice_in_dim(cells, 0, width, axis=dim)
        tail = lax.slice_in_dim(cells, cells.shape[dim] - width, cells.shape[dim], axis=dim)
        cells = jnp.concatenate(
            [
                lax.ppermute(tail, axis, [(i, (i + 1) % count) for i in range(count)]),
                cells,
                lax.ppermute(head, axis, [((i + 1) % count, i) for i in range(count)]),
            ],
            axis=dim,
        )
    return cells


def interpolate(own_tile, packed):
    cell_rows = packed[0][None, :] * BLK + packed[1:5]
    picked = jnp.take(own_tile, cell_rows.reshape(-1), axis=0).astype(F32)
    picked = picked.reshape(4, cell_rows.shape[1], own_tile.shape[1])
    frac_lat = (packed[5].astype(F32) + 0.5) / FRAC
    frac_lon = (packed[6].astype(F32) + 0.5) / FRAC
    weights = jnp.stack(
        [
            (1.0 - frac_lat) * (1.0 - frac_lon),
            frac_lat * (1.0 - frac_lon),
            (1.0 - frac_lat) * frac_lon,
            frac_lat * frac_lon,
        ]
    )
    return jnp.sum(weights[:, :, None] * picked, axis=0).astype(BF16)


def place_columns(values, counts, columns):
    slot_ends = jnp.cumsum(counts)
    starts = slot_ends - counts
    column = jnp.arange(columns, dtype=jnp.int32)
    slot_index = jnp.sum((slot_ends[None, :] <= column[:, None]).astype(jnp.int32), axis=1)
    onehot = slot_index[:, None] == jnp.arange(SLOTS, dtype=jnp.int32)[None, :]
    offset = column - jnp.sum(jnp.where(onehot, starts[None, :], 0), axis=1)
    flat_index = slot_index * values.shape[1] + offset
    return jnp.take(values.reshape(-1, values.shape[-1]), flat_index, axis=0)


def exchanging(fields, req_block, req_stencil, req_frac, req_count, legendre):
    lat_rows, lon_cols, channels = fields.shape
    count = lax.axis_size("lon")
    waves_total = legendre.shape[0] * count * lax.axis_size("lat")
    packed = jnp.concatenate(
        [req_block[0, 0][:, None, :], req_stencil[0, 0], req_frac[0, 0]], axis=1
    )
    counts = req_count[0, 0]
    widened = padded(fields, (("lon", 1),), lon_cols)
    slot_values = []
    for slot_index in range(SLOTS):
        owner_tile = widened[:, slot_index * lon_cols : (slot_index + 1) * lon_cols, :].reshape(
            -1, channels
        )
        slot_values.append(interpolate(owner_tile, packed[slot_index]))
    departed = place_columns(jnp.stack(slot_values), counts, lat_rows * lon_cols)
    departed = departed.reshape(lat_rows, lon_cols, channels)
    lon_total = lon_cols * count
    spectra = jnp.einsum(
        "kx,yxc->ykc",
        hartley_table(waves_total, lon_total),
        lax.all_to_all(departed, "lon", split_axis=0, concat_axis=1, tiled=True),
        preferred_element_type=F32,
    )
    fourier = lax.all_to_all(spectra.astype(BF16), "lon", split_axis=1, concat_axis=0, tiled=True)
    gathered = lax.all_to_all(fourier, "lat", split_axis=1, concat_axis=0, tiled=True)
    projected = jnp.einsum("kyn,ykc->knc", legendre, gathered, preferred_element_type=F32)
    degrees = legendre.shape[2]
    degree = jnp.arange(degrees, dtype=F32)
    factor = 1.0 / (1.0 + 4.0 * degree * (degree + 1.0) / (degrees * (degrees + 1)))
    return projected * factor[None, :, None]


def local(fields, req_block, req_stencil, req_frac, req_count, legendre):
    count = lax.axis_size("lon")
    lon_cols = fields.shape[1]
    sector_waves = legendre.shape[0] * lax.axis_size("lat")
    bands = lax.axis_size("lat")
    fits = count * lon_cols <= lon_cols + sector_waves
    fits = fits and bands & (bands - 1) == 0 and count & (count - 1) == 0
    plan = gathering if fits else exchanging
    return plan(fields, req_block, req_stencil, req_frac, req_count, legendre)


def solution(mesh):
    return jax.shard_map(
        local,
        mesh=mesh,
        in_specs=(
            P("lat", "lon", None),
            P("lat", "lon", None, None),
            P("lat", "lon", None, None, None),
            P("lat", "lon", None, None, None),
            P("lat", "lon", None),
            P(("lon", "lat"), None, None),
        ),
        out_specs=P(("lon", "lat"), None, None),
        check_vma=False,
    )
```

```python
import functools
import math

import jax
import jax.numpy as jnp
import numpy as np
from jax import lax
from jax.experimental import pallas as pl
from jax.experimental.pallas import tpu as pltpu
from jax.sharding import PartitionSpec as P

BLK = 16
FRAC = 16
SLOTS = 3
LANES = 128
SPAN = 2 * LANES
UNROLL = 4
F32 = jnp.float32
BF16 = jnp.bfloat16


def hartley_table(waves, lon_total):
    wave_index = jnp.arange(waves, dtype=jnp.int32)
    lon_index = jnp.arange(lon_total, dtype=jnp.int32)
    phase_index = wave_index[:, None] * lon_index[None, :] % lon_total
    phase_angle = 2.0 * math.pi / lon_total * phase_index.astype(F32)
    return ((jnp.cos(phase_angle) + jnp.sin(phase_angle)) / math.sqrt(lon_total)).astype(BF16)


def hartley_constant(waves, lon_total):
    phase_index = np.arange(waves)[:, None] * np.arange(lon_total)[None, :] % lon_total
    phase_angle = np.float32(2.0 * math.pi / lon_total) * phase_index.astype(np.float32)
    table = (np.cos(phase_angle) + np.sin(phase_angle)) / np.float32(math.sqrt(lon_total))
    return jnp.asarray(table.astype(BF16))


def chunk_list(channels):
    half = channels // 2
    return ((0, half), (half, half))


def pack_body(chunks, blocks, counts, fields, block, stencil, frac, *rest):
    outs, (wide, *held, done) = rest[: len(chunks)], rest[len(chunks) :]
    copies = [
        pltpu.make_async_copy(given, kept, done.at[number])
        for number, (given, kept) in enumerate(zip((counts, fields, block, stencil, frac), held, strict=True))
    ]
    for copy in copies:
        copy.start()
    for copy in copies:
        copy.wait()
    counts, fields, block, stencil, frac = held
    cells = blocks * BLK
    cap = block.shape[1]
    wide[...] = fields[...].astype(F32)
    lane = lax.broadcasted_iota(jnp.int32, (blocks, LANES), 1)
    for out, (first, width) in zip(outs, chunks, strict=True):
        groups = LANES // width
        planes = BLK // groups
        for plane in range(planes):
            total = None
            for group in range(groups):
                rows = wide[pl.ds(group * planes + plane, blocks, stride=BLK), :]
                shift = (group * width - first) % LANES
                if shift:
                    rows = pltpu.roll(rows, shift, 1)
                total = rows if total is None else jnp.where(lane >= group * width, rows, total)
            out[plane * blocks : (plane + 1) * blocks, :] = total.astype(BF16)
    starts = (0, counts[0], counts[0] + counts[1])
    column = lax.broadcasted_iota(jnp.int32, (8, cells), 1)
    row = lax.broadcasted_iota(jnp.int32, (8, cells), 0)
    slot = (column >= starts[1]).astype(jnp.int32) + (column >= starts[2]).astype(jnp.int32)
    placed = slot.astype(F32)
    for index in range(SLOTS):
        listed = jnp.concatenate(
            [
                block[index : index + 1, :].astype(F32),
                stencil[index].astype(F32),
                frac[index].astype(F32),
                jnp.zeros((1, cap), F32),
            ],
            axis=0,
        )
        listed = jnp.concatenate([listed, jnp.zeros((8, cells - cap), F32)], axis=1)
        if index:
            listed = pltpu.roll(listed, starts[index], 1)
        placed = jnp.where((slot == index) & (row < 7), listed, placed)
    base = outs[0].shape[0] - cells // LANES * 8
    for span in range(cells // SPAN):
        pair = jnp.concatenate(
            [
                placed[:, span * SPAN : span * SPAN + LANES],
                placed[:, span * SPAN + LANES : (span + 1) * SPAN],
            ],
            axis=0,
        )
        outs[0][base + span * 16 : base + (span + 1) * 16, :] = pair.astype(BF16)


def interp_body(count, bands, width, blocks, lead, late, far, reach, here, *rest):
    tiles, rest = rest[: len(reach)], rest[len(reach) :]
    if not lead:
        (params, ends), rest = rest[:2], rest[2:]
    if late:
        (given, table), rest = rest[:2], rest[2:]
        outs, rest, (grid, spectra) = rest[:bands], rest[bands:-2], rest[-2:]
    else:
        grid, *rest = rest
    if lead:
        params, ends, flipped, work = rest
    else:
        flipped, work = rest
    me = here[0]
    groups = LANES // width
    planes = BLK // groups
    owners = [jnp.bitwise_xor(me, step) for step, _ in reach]

    def distant(other):
        step = jnp.bitwise_xor(me, other)
        return functools.reduce(jnp.logical_or, [step == one for one in far], jnp.bool_(False))

    def present(number):
        return (jnp.abs(me - owners[number]) <= count // 2) == reach[number][1]

    def take(tile, owner):
        for plane in range(planes):
            rows = tile[plane * blocks : (plane + 1) * blocks, :]
            flipped[owner, plane * LANES : (plane + 1) * LANES, :] = rows.T

    if lead:
        for number, tile in enumerate(tiles):

            @pl.when(present(number))
            def _(number=number, tile=tile):
                params[owners[number]] = tile[planes * blocks :, :]

        for tile in range(count):
            ends[tile, 0] = 0

            @pl.when(late | jnp.logical_not(distant(tile)))
            def _(tile=tile):
                rows = params[tile].astype(F32)
                which = lax.broadcasted_iota(jnp.int32, rows.shape, 0) % 8 == 7
                for index in range(SLOTS):
                    listed = jnp.where(which & (rows <= index), 1.0, 0.0)
                    ends[tile, index + 1] = jnp.sum(listed).astype(jnp.int32)

    if late:
        grid[...] = given[...]
    else:
        grid[...] = jnp.zeros_like(grid)

    block_row = lax.broadcasted_iota(jnp.int32, (blocks, SPAN), 0).astype(F32)
    cell_row = lax.broadcasted_iota(jnp.int32, (BLK, SPAN), 0).astype(F32)

    def wanted(owner, index):
        target = lax.rem(owner - index + 1 + count, count)
        if not lead:
            return jnp.bool_(True)
        either = distant(target) | distant(owner)
        return either if late else jnp.logical_not(either)

    spans = blocks * BLK // SPAN
    entries = jnp.int32(0)
    for number, tile in enumerate(tiles):
        owner = owners[number]
        asked = [present(number) & wanted(owner, index) for index in range(SLOTS)]

        @pl.when(functools.reduce(jnp.logical_or, asked))
        def _(tile=tile, owner=owner):
            take(tile, owner)

        for index in range(SLOTS):
            target = lax.rem(owner - index + 1 + count, count)
            target = jnp.where(asked[index], target, 0)
            low = ends[target, index]
            high = ends[target, index + 1]
            first = low // SPAN
            extra = (high + SPAN - 1) // SPAN - first
            extra = jnp.where(asked[index] & (high > low), extra, 0)
            code = ((owner * count + target) * SLOTS + index) * spans + first

            def enter(span, _, code=code, entries=entries):
                work[entries + span] = code + span
                return 0

            lax.fori_loop(0, extra, enter, 0)
            entries = entries + extra

    def entry_step(entry):
        code = work[jnp.minimum(entry, entries - 1)]
        span = lax.rem(code, spans)
        code = code // spans
        index = jnp.where(entry < entries, lax.rem(code, SLOTS), -1)
        code = code // SLOTS
        target, owner = lax.rem(code, count), code // count
        both = params[target, pl.ds(pl.multiple_of(span * 16, 16), 16), :].astype(F32)

        def line(i):
            return jnp.concatenate([both[i : i + 1, :], both[8 + i : 9 + i, :]], axis=1)

        key = jnp.where(line(7) == index.astype(F32), line(0), -1.0)
        onehot = jnp.where(block_row == key, 1.0, 0.0).astype(BF16)
        f_lat = (line(5) + 0.5) / FRAC
        f_lon = (line(6) + 0.5) / FRAC
        corners = (
            (1.0 - f_lat) * (1.0 - f_lon),
            f_lat * (1.0 - f_lon),
            (1.0 - f_lat) * f_lon,
            f_lat * f_lon,
        )
        weight = jnp.zeros((BLK, SPAN), F32)
        for corner in range(4):
            weight += jnp.where(cell_row == line(1 + corner), corners[corner], 0.0)
        total = jnp.zeros((width, SPAN), F32)
        for plane in range(planes):
            picked = jnp.dot(
                flipped[owner, plane * LANES : (plane + 1) * LANES, :],
                onehot,
                preferred_element_type=F32,
            )
            for group in range(groups):
                cell = group * planes + plane
                total += (
                    weight[cell : cell + 1, :] * picked[group * width : (group + 1) * width, :]
                )
        return span, pl.multiple_of(target * LANES, LANES), total.astype(BF16)

    def step(number, _):
        found = [entry_step(number * UNROLL + inner) for inner in range(UNROLL)]
        for span, place, total in found:
            for half in range(2):
                rows = pl.ds(pl.multiple_of((2 * span + half) * width, width), width)
                grid[rows, pl.ds(place, LANES)] += total[:, half * LANES : (half + 1) * LANES]
        return 0

    lax.fori_loop(0, (entries + UNROLL - 1) // UNROLL, step, 0)

    if late:
        spectra[...] = lax.dot_general(
            table[...], grid[...], (((1,), (1,)), ((), ())), preferred_element_type=F32
        ).astype(BF16)
        waves = outs[0].shape[0]
        for shift, out in enumerate(outs):
            start = pl.multiple_of(jnp.bitwise_xor(here[1], shift) * waves, 16)
            out[...] = spectra[pl.ds(start, waves), :]


def spread_rows(piece, row, first, width):
    groups = LANES // width
    tile, group = row // groups, row % groups
    values = piece[:, tile * LANES : (tile + 1) * LANES].astype(F32)
    turn = (first - group * width) % LANES
    return pltpu.roll(values, turn, 1) if turn else values


def collect_body(chunks, bands, lat_rows, here, *rest):
    pieces, gathered = rest[:-1], rest[-1]
    waves = pieces[0].shape[0]
    lane = lax.broadcasted_iota(jnp.int32, (waves, LANES), 1)
    for shift in range(bands):
        source = jnp.bitwise_xor(here[1], shift)
        for row in range(lat_rows):
            total = None
            for part, (first, width) in enumerate(chunks):
                values = spread_rows(pieces[part * bands + shift], row, first, width)
                total = values if total is None else jnp.where(lane >= first, values, total)
            start = pl.multiple_of((source * lat_rows + row) * waves, 8)
            gathered[pl.ds(start, waves), :] = total


def final_body(last, bands, lat_rows, per_step, per_copy, here, legendre, early, *rest):
    pieces, (out, gathered, factor, staged, done) = rest[:bands], rest[bands:]
    waves, lat_total, degrees = legendre.shape
    first, width = last
    degree = lax.broadcasted_iota(jnp.int32, factor.shape, 0).astype(F32)
    factor[...] = 1.0 / (1.0 + 4.0 * degree * (degree + 1.0) / (degrees * (degrees + 1)))
    lane = lax.broadcasted_iota(jnp.int32, (waves, LANES), 1)
    for shift in range(bands):
        source = jnp.bitwise_xor(here[1], shift)
        for row in range(lat_rows):
            values = spread_rows(pieces[shift], row, first, width)
            rows = pl.ds(pl.multiple_of((source * lat_rows + row) * waves, 8), waves)
            gathered[rows, :] = jnp.where(lane >= first, values, early[rows, :])

    def step(number, _):
        for inner in range(per_step):
            wave = number * per_step + inner
            column = gathered[pl.ds(wave, lat_total, stride=waves), :].astype(BF16)
            projected = lax.dot_general(
                legendre[wave], column, (((0,), (0,)), ((), ())), preferred_element_type=F32
            )
            staged[wave] = projected * factor[...]
            if (inner + 1) % per_copy == 0:
                rows = pl.ds(wave + 1 - per_copy, per_copy)
                pltpu.make_async_copy(staged.at[rows], out.at[rows], done).start()
        return 0

    lax.fori_loop(0, waves // per_step, step, 0)
    pltpu.make_async_copy(staged, out, done).wait()


VMEM = pl.BlockSpec(memory_space=pltpu.VMEM)
SMEM = pl.BlockSpec(memory_space=pltpu.SMEM)
ANY = pl.BlockSpec(memory_space=pl.ANY)


def limit(mib):
    return pltpu.CompilerParams(vmem_limit_bytes=mib * 2**20)


def cost(flops):
    return pl.CostEstimate(flops=flops, bytes_accessed=10**6, transcendentals=0)


def gathering(fields, req_block, req_stencil, req_frac, req_count, legendre):
    lat_rows, lon_cols, channels = fields.shape
    waves, lat_total, degrees = legendre.shape
    count, bands = lax.axis_size("lon"), lax.axis_size("lat")
    cells = lat_rows * lon_cols
    blocks = cells // BLK
    lon_total = lon_cols * count
    sector_waves = waves * bands
    chunks = chunk_list(channels)
    me = lax.axis_index("lon")
    here = jnp.stack([me, lax.axis_index("lat")]).astype(jnp.int32)

    table = hartley_constant(sector_waves * count, lon_total)
    table = lax.dynamic_slice_in_dim(table, me * sector_waves, sector_waves, axis=0)

    tile_rows = [blocks * BLK * width // LANES for _, width in chunks]
    tile_rows[0] += cells // LANES * 8
    packed = pl.pallas_call(
        functools.partial(pack_body, chunks, blocks),
        out_shape=[jax.ShapeDtypeStruct((rows, LANES), BF16) for rows in tile_rows],
        in_specs=[pl.BlockSpec(memory_space=pltpu.HBM)] * 5,
        out_specs=[VMEM] * len(tile_rows),
        scratch_shapes=[
            pltpu.VMEM((cells, channels), F32),
            pltpu.SMEM(req_count.shape[2:], jnp.int32),
            pltpu.VMEM((cells, channels), BF16),
            pltpu.VMEM(req_block.shape[2:], jnp.int32),
            pltpu.VMEM(req_stencil.shape[2:], jnp.int32),
            pltpu.VMEM(req_frac.shape[2:], jnp.int32),
            pltpu.SemaphoreType.DMA((5,)),
        ],
        compiler_params=limit(63),
        name="pack",
    )(req_count[0, 0], fields.reshape(cells, channels), req_block[0, 0], req_stencil[0, 0], req_frac[0, 0])

    near = [(i, i ^ step) for step in range(count) for i in range(count) if abs(i - (i ^ step)) <= count // 2]

    def after(tile, others):
        return lax.optimization_barrier((tile, *others))[0] if others else tile

    def exchange(tile, step, others=()):
        return lax.ppermute(after(tile, others), "lon", [pair for pair in near if pair[0] ^ pair[1] == step])

    def relay(tile, step):
        pairs = [(i ^ 1, i) for i in range(count) if (i, i ^ step) not in near]
        return lax.ppermute(tile, "lon", pairs)

    far = [step for step in range(count) if any((i, i ^ step) not in near for i in range(count))]
    parts = []
    params = ends = None
    ahead = moved = ()
    for number, (first, width) in enumerate(chunks):
        lead = number == 0
        tile = packed[number]
        near_tiles = {step: exchange(tile, step, ahead) for step in range(1, count) if step not in far}
        ahead = tuple(near_tiles.values())
        far_tiles = [(exchange(tile, step, ahead), step, True) for step in far]
        passed = [relay(near_tiles[step ^ 1], step) for step in far]
        far_tiles += [(got, step, False) for got, step in zip(passed, far, strict=True)]
        soon = [(tile, 0, True)] + [(got, step, True) for step, got in near_tiles.items()]
        last = soon + far_tiles if lead else far_tiles
        scratch = [
            pltpu.VMEM((count, BLK * width, blocks), BF16),
            pltpu.SMEM((count * SLOTS * (cells // SPAN + 1),), jnp.int32),
        ]
        grid = jax.ShapeDtypeStruct((lat_rows * width, lon_total), BF16)
        listed = [
            jax.ShapeDtypeStruct((count, cells // LANES * 8, LANES), BF16),
            jax.ShapeDtypeStruct((count, SLOTS + 1), jnp.int32),
        ]
        given = [] if lead else [params, ends]
        given_specs = [] if lead else [VMEM, SMEM]
        kept = [pltpu.VMEM(listed[0].shape, BF16), pltpu.SMEM(listed[1].shape, jnp.int32)]
        grid = pl.pallas_call(
            functools.partial(interp_body, count, bands, width, blocks, lead, False, far, [one[1:] for one in soon]),
            out_shape=grid,
            in_specs=[SMEM] + [VMEM] * len(soon) + given_specs,
            out_specs=VMEM,
            scratch_shapes=(kept if lead else []) + scratch,
            compiler_params=limit(24),
            cost_estimate=cost(width * 10**9),
            name="early",
        )(here, *[one[0] for one in soon], *given)
        ahead = (grid, *[got for got, _, _ in far_tiles])
        grid = after(grid, moved)
        results = pl.pallas_call(
            functools.partial(interp_body, count, bands, width, blocks, lead, True, far, [one[1:] for one in last]),
            out_shape=[jax.ShapeDtypeStruct((waves, lat_rows * width), BF16)] * bands
            + (listed if lead else []),
            in_specs=[SMEM] + [VMEM] * len(last) + given_specs + [VMEM, VMEM],
            out_specs=[VMEM] * bands + ([VMEM, SMEM] if lead else []),
            scratch_shapes=scratch
            + [
                pltpu.VMEM(grid.shape, BF16),
                pltpu.VMEM((sector_waves, lat_rows * width), BF16),
            ],
            compiler_params=limit(24),
            cost_estimate=cost(width * 5 * 10**7),
            name="late",
        )(here, *[one[0] for one in last], *given, grid, table)
        if lead:
            params, ends = results[bands:]
        pieces = [results[0]]
        for shift in range(1, bands):
            pieces.append(lax.ppermute(results[shift], "lat", [(i, i ^ shift) for i in range(bands)]))
        parts.append(pieces)
        moved = pieces[2:6]

    gathered = jax.ShapeDtypeStruct((lat_total * waves, channels), F32)
    early = [piece for pieces in parts[:-1] for piece in pieces]
    early = pl.pallas_call(
        functools.partial(collect_body, chunks[:-1], bands, lat_rows),
        out_shape=gathered,
        in_specs=[SMEM] + [VMEM] * len(early),
        out_specs=VMEM,
        compiler_params=limit(16),
        cost_estimate=cost(10**9),
        name="collect",
    )(here, *early)
    per_step = math.gcd(waves, 16)
    return pl.pallas_call(
        functools.partial(final_body, chunks[-1], bands, lat_rows, per_step, math.gcd(per_step, 4)),
        out_shape=jax.ShapeDtypeStruct((waves, degrees, channels), F32),
        in_specs=[SMEM] + [VMEM] * (bands + 2),
        out_specs=ANY,
        scratch_shapes=[
            pltpu.VMEM(gathered.shape, F32),
            pltpu.VMEM((degrees, channels), F32),
            pltpu.VMEM((waves, degrees, channels), F32),
            pltpu.SemaphoreType.DMA,
        ],
        compiler_params=limit(28),
        name="final",
    )(here, legendre, early, *parts[-1])


def padded(cells, sides, width):
    for axis, dim in sides:
        count = lax.axis_size(axis)
        head = lax.slice_in_dim(cells, 0, width, axis=dim)
        tail = lax.slice_in_dim(cells, cells.shape[dim] - width, cells.shape[dim], axis=dim)
        cells = jnp.concatenate(
            [
                lax.ppermute(tail, axis, [(i, (i + 1) % count) for i in range(count)]),
                cells,
                lax.ppermute(head, axis, [((i + 1) % count, i) for i in range(count)]),
            ],
            axis=dim,
        )
    return cells


def interpolate(own_tile, packed):
    cell_rows = packed[0][None, :] * BLK + packed[1:5]
    picked = jnp.take(own_tile, cell_rows.reshape(-1), axis=0).astype(F32)
    picked = picked.reshape(4, cell_rows.shape[1], own_tile.shape[1])
    frac_lat = (packed[5].astype(F32) + 0.5) / FRAC
    frac_lon = (packed[6].astype(F32) + 0.5) / FRAC
    weights = jnp.stack(
        [
            (1.0 - frac_lat) * (1.0 - frac_lon),
            frac_lat * (1.0 - frac_lon),
            (1.0 - frac_lat) * frac_lon,
            frac_lat * frac_lon,
        ]
    )
    return jnp.sum(weights[:, :, None] * picked, axis=0).astype(BF16)


def place_columns(values, counts, columns):
    slot_ends = jnp.cumsum(counts)
    starts = slot_ends - counts
    column = jnp.arange(columns, dtype=jnp.int32)
    slot_index = jnp.sum((slot_ends[None, :] <= column[:, None]).astype(jnp.int32), axis=1)
    onehot = slot_index[:, None] == jnp.arange(SLOTS, dtype=jnp.int32)[None, :]
    offset = column - jnp.sum(jnp.where(onehot, starts[None, :], 0), axis=1)
    flat_index = slot_index * values.shape[1] + offset
    return jnp.take(values.reshape(-1, values.shape[-1]), flat_index, axis=0)


def exchanging(fields, req_block, req_stencil, req_frac, req_count, legendre):
    lat_rows, lon_cols, channels = fields.shape
    count = lax.axis_size("lon")
    waves_total = legendre.shape[0] * count * lax.axis_size("lat")
    packed = jnp.concatenate(
        [req_block[0, 0][:, None, :], req_stencil[0, 0], req_frac[0, 0]], axis=1
    )
    counts = req_count[0, 0]
    widened = padded(fields, (("lon", 1),), lon_cols)
    slot_values = []
    for slot_index in range(SLOTS):
        owner_tile = widened[:, slot_index * lon_cols : (slot_index + 1) * lon_cols, :].reshape(
            -1, channels
        )
        slot_values.append(interpolate(owner_tile, packed[slot_index]))
    departed = place_columns(jnp.stack(slot_values), counts, lat_rows * lon_cols)
    departed = departed.reshape(lat_rows, lon_cols, channels)
    lon_total = lon_cols * count
    spectra = jnp.einsum(
        "kx,yxc->ykc",
        hartley_table(waves_total, lon_total),
        lax.all_to_all(departed, "lon", split_axis=0, concat_axis=1, tiled=True),
        preferred_element_type=F32,
    )
    fourier = lax.all_to_all(spectra.astype(BF16), "lon", split_axis=1, concat_axis=0, tiled=True)
    gathered = lax.all_to_all(fourier, "lat", split_axis=1, concat_axis=0, tiled=True)
    projected = jnp.einsum("kyn,ykc->knc", legendre, gathered, preferred_element_type=F32)
    degrees = legendre.shape[2]
    degree = jnp.arange(degrees, dtype=F32)
    factor = 1.0 / (1.0 + 4.0 * degree * (degree + 1.0) / (degrees * (degrees + 1)))
    return projected * factor[None, :, None]


def local(fields, req_block, req_stencil, req_frac, req_count, legendre):
    count = lax.axis_size("lon")
    lon_cols = fields.shape[1]
    sector_waves = legendre.shape[0] * lax.axis_size("lat")
    bands = lax.axis_size("lat")
    fits = count * lon_cols <= lon_cols + sector_waves
    fits = fits and bands & (bands - 1) == 0 and count & (count - 1) == 0
    plan = gathering if fits else exchanging
    return plan(fields, req_block, req_stencil, req_frac, req_count, legendre)


def solution(mesh):
    return jax.shard_map(
        local,
        mesh=mesh,
        in_specs=(
            P("lat", "lon", None),
            P("lat", "lon", None, None),
            P("lat", "lon", None, None, None),
            P("lat", "lon", None, None, None),
            P("lat", "lon", None),
            P(("lon", "lat"), None, None),
        ),
        out_specs=P(("lon", "lat"), None, None),
        check_vma=False,
    )
```

```python
import functools
import math

import jax
import jax.numpy as jnp
import numpy as np
from jax import lax
from jax.experimental import pallas as pl
from jax.experimental.pallas import tpu as pltpu
from jax.sharding import PartitionSpec as P

BLK = 16
FRAC = 16
SLOTS = 3
LANES = 128
SPAN = 2 * LANES
UNROLL = 5
F32 = jnp.float32
BF16 = jnp.bfloat16


def hartley_table(waves, lon_total):
    wave_index = jnp.arange(waves, dtype=jnp.int32)
    lon_index = jnp.arange(lon_total, dtype=jnp.int32)
    phase_index = wave_index[:, None] * lon_index[None, :] % lon_total
    phase_angle = 2.0 * math.pi / lon_total * phase_index.astype(F32)
    return ((jnp.cos(phase_angle) + jnp.sin(phase_angle)) / math.sqrt(lon_total)).astype(BF16)


def hartley_constant(waves, lon_total):
    phase_index = np.arange(waves)[:, None] * np.arange(lon_total)[None, :] % lon_total
    phase_angle = np.float32(2.0 * math.pi / lon_total) * phase_index.astype(np.float32)
    table = (np.cos(phase_angle) + np.sin(phase_angle)) / np.float32(math.sqrt(lon_total))
    return jnp.asarray(table.astype(BF16))


def chunk_list(channels):
    half = channels // 2
    return ((0, half), (half, half))


def pack_body(chunks, blocks, counts, fields, block, stencil, frac, *rest):
    outs, (wide, *held, done) = rest[: len(chunks)], rest[len(chunks) :]
    copies = [
        pltpu.make_async_copy(given, kept, done.at[number])
        for number, (given, kept) in enumerate(zip((counts, fields, block, stencil, frac), held, strict=True))
    ]
    for copy in copies:
        copy.start()
    for copy in copies:
        copy.wait()
    counts, fields, block, stencil, frac = held
    cells = blocks * BLK
    cap = block.shape[1]
    wide[...] = fields[...].astype(F32)
    lane = lax.broadcasted_iota(jnp.int32, (blocks, LANES), 1)
    for out, (first, width) in zip(outs, chunks, strict=True):
        groups = LANES // width
        planes = BLK // groups
        for plane in range(planes):
            total = None
            for group in range(groups):
                rows = wide[pl.ds(group * planes + plane, blocks, stride=BLK), :]
                shift = (group * width - first) % LANES
                if shift:
                    rows = pltpu.roll(rows, shift, 1)
                total = rows if total is None else jnp.where(lane >= group * width, rows, total)
            out[plane * blocks : (plane + 1) * blocks, :] = total.astype(BF16)
    starts = (0, counts[0], counts[0] + counts[1])
    column = lax.broadcasted_iota(jnp.int32, (8, cells), 1)
    row = lax.broadcasted_iota(jnp.int32, (8, cells), 0)
    slot = (column >= starts[1]).astype(jnp.int32) + (column >= starts[2]).astype(jnp.int32)
    placed = slot.astype(F32)
    for index in range(SLOTS):
        listed = jnp.concatenate(
            [
                block[index : index + 1, :].astype(F32),
                stencil[index].astype(F32),
                frac[index].astype(F32),
                jnp.zeros((1, cap), F32),
            ],
            axis=0,
        )
        listed = jnp.concatenate([listed, jnp.zeros((8, cells - cap), F32)], axis=1)
        if index:
            listed = pltpu.roll(listed, starts[index], 1)
        placed = jnp.where((slot == index) & (row < 7), listed, placed)
    base = outs[0].shape[0] - cells // LANES * 8
    for span in range(cells // SPAN):
        pair = jnp.concatenate(
            [
                placed[:, span * SPAN : span * SPAN + LANES],
                placed[:, span * SPAN + LANES : (span + 1) * SPAN],
            ],
            axis=0,
        )
        outs[0][base + span * 16 : base + (span + 1) * 16, :] = pair.astype(BF16)


def interp_body(count, bands, width, blocks, lead, late, far, reach, here, *rest):
    tiles, rest = rest[: len(reach)], rest[len(reach) :]
    if not lead:
        (params, ends), rest = rest[:2], rest[2:]
    if late:
        (given, table), rest = rest[:2], rest[2:]
        outs, rest, (grid, spectra) = rest[:bands], rest[bands:-2], rest[-2:]
    else:
        grid, *rest = rest
    if lead:
        params, ends, flipped, work = rest
    else:
        flipped, work = rest
    me = here[0]
    groups = LANES // width
    planes = BLK // groups
    owners = [jnp.bitwise_xor(me, step) for step, _ in reach]

    def distant(other):
        step = jnp.bitwise_xor(me, other)
        return functools.reduce(jnp.logical_or, [step == one for one in far], jnp.bool_(False))

    def present(number):
        return (jnp.abs(me - owners[number]) <= count // 2) == reach[number][1]

    def take(tile, owner):
        for plane in range(planes):
            rows = tile[plane * blocks : (plane + 1) * blocks, :]
            flipped[owner, plane * LANES : (plane + 1) * LANES, :] = rows.T

    if lead:
        for number, tile in enumerate(tiles):

            @pl.when(present(number))
            def _(number=number, tile=tile):
                params[owners[number]] = tile[planes * blocks :, :]

        for tile in range(count):
            ends[tile, 0] = 0

            @pl.when(late | jnp.logical_not(distant(tile)))
            def _(tile=tile):
                rows = params[tile].astype(F32)
                which = lax.broadcasted_iota(jnp.int32, rows.shape, 0) % 8 == 7
                for index in range(SLOTS):
                    listed = jnp.where(which & (rows <= index), 1.0, 0.0)
                    ends[tile, index + 1] = jnp.sum(listed).astype(jnp.int32)

    if late:
        grid[...] = given[...]
    else:
        grid[...] = jnp.zeros_like(grid)

    block_row = lax.broadcasted_iota(jnp.int32, (blocks, SPAN), 0).astype(F32)
    cell_row = lax.broadcasted_iota(jnp.int32, (BLK, SPAN), 0).astype(F32)

    def wanted(owner, index):
        target = lax.rem(owner - index + 1 + count, count)
        if not lead:
            return jnp.bool_(True)
        either = distant(target) | distant(owner)
        return either if late else jnp.logical_not(either)

    spans = blocks * BLK // SPAN
    entries = jnp.int32(0)
    for number, tile in enumerate(tiles):
        owner = owners[number]
        asked = [present(number) & wanted(owner, index) for index in range(SLOTS)]

        @pl.when(functools.reduce(jnp.logical_or, asked))
        def _(tile=tile, owner=owner):
            take(tile, owner)

        for index in range(SLOTS):
            target = lax.rem(owner - index + 1 + count, count)
            target = jnp.where(asked[index], target, 0)
            low = ends[target, index]
            high = ends[target, index + 1]
            first = low // SPAN
            extra = (high + SPAN - 1) // SPAN - first
            extra = jnp.where(asked[index] & (high > low), extra, 0)
            code = ((owner * count + target) * SLOTS + index) * spans + first

            def enter(span, _, code=code, entries=entries):
                work[entries + span] = code + span
                return 0

            lax.fori_loop(0, extra, enter, 0)
            entries = entries + extra

    def entry_step(entry):
        code = work[jnp.minimum(entry, entries - 1)]
        span = lax.rem(code, spans)
        code = code // spans
        index = jnp.where(entry < entries, lax.rem(code, SLOTS), -1)
        code = code // SLOTS
        target, owner = lax.rem(code, count), code // count
        both = params[target, pl.ds(pl.multiple_of(span * 16, 16), 16), :].astype(F32)

        def line(i):
            return jnp.concatenate([both[i : i + 1, :], both[8 + i : 9 + i, :]], axis=1)

        key = jnp.where(line(7) == index.astype(F32), line(0), -1.0)
        onehot = jnp.where(block_row == key, 1.0, 0.0).astype(BF16)
        f_lat = (line(5) + 0.5) / FRAC
        f_lon = (line(6) + 0.5) / FRAC
        corners = (
            (1.0 - f_lat) * (1.0 - f_lon),
            f_lat * (1.0 - f_lon),
            (1.0 - f_lat) * f_lon,
            f_lat * f_lon,
        )
        weight = jnp.zeros((BLK, SPAN), F32)
        for corner in range(4):
            weight += jnp.where(cell_row == line(1 + corner), corners[corner], 0.0)
        total = jnp.zeros((width, SPAN), F32)
        for plane in range(planes):
            picked = jnp.dot(
                flipped[owner, plane * LANES : (plane + 1) * LANES, :],
                onehot,
                preferred_element_type=F32,
            )
            for group in range(groups):
                cell = group * planes + plane
                total += (
                    weight[cell : cell + 1, :] * picked[group * width : (group + 1) * width, :]
                )
        return span, pl.multiple_of(target * LANES, LANES), total.astype(BF16)

    def step(number, _):
        found = [entry_step(number * UNROLL + inner) for inner in range(UNROLL)]
        for span, place, total in found:
            for half in range(2):
                rows = pl.ds(pl.multiple_of((2 * span + half) * width, width), width)
                grid[rows, pl.ds(place, LANES)] += total[:, half * LANES : (half + 1) * LANES]
        return 0

    lax.fori_loop(0, (entries + UNROLL - 1) // UNROLL, step, 0)

    if late:
        spectra[...] = lax.dot_general(
            table[...], grid[...], (((1,), (1,)), ((), ())), preferred_element_type=F32
        ).astype(BF16)
        waves = outs[0].shape[0]
        for shift, out in enumerate(outs):
            start = pl.multiple_of(jnp.bitwise_xor(here[1], shift) * waves, 16)
            out[...] = spectra[pl.ds(start, waves), :]


def spread_rows(piece, row, first, width):
    groups = LANES // width
    tile, group = row // groups, row % groups
    values = piece[:, tile * LANES : (tile + 1) * LANES].astype(F32)
    turn = (first - group * width) % LANES
    return pltpu.roll(values, turn, 1) if turn else values


def collect_body(chunks, bands, lat_rows, here, *rest):
    pieces, gathered = rest[:-1], rest[-1]
    waves = pieces[0].shape[0]
    lane = lax.broadcasted_iota(jnp.int32, (waves, LANES), 1)
    for shift in range(bands):
        source = jnp.bitwise_xor(here[1], shift)
        for row in range(lat_rows):
            total = None
            for part, (first, width) in enumerate(chunks):
                values = spread_rows(pieces[part * bands + shift], row, first, width)
                total = values if total is None else jnp.where(lane >= first, values, total)
            start = pl.multiple_of((source * lat_rows + row) * waves, 8)
            gathered[pl.ds(start, waves), :] = total


def final_body(last, bands, lat_rows, per_step, per_copy, here, legendre, early, *rest):
    pieces, (out, gathered, factor, staged, done) = rest[:bands], rest[bands:]
    waves, lat_total, degrees = legendre.shape
    first, width = last
    degree = lax.broadcasted_iota(jnp.int32, factor.shape, 0).astype(F32)
    factor[...] = 1.0 / (1.0 + 4.0 * degree * (degree + 1.0) / (degrees * (degrees + 1)))
    lane = lax.broadcasted_iota(jnp.int32, (waves, LANES), 1)
    for shift in range(bands):
        source = jnp.bitwise_xor(here[1], shift)
        for row in range(lat_rows):
            values = spread_rows(pieces[shift], row, first, width)
            rows = pl.ds(pl.multiple_of((source * lat_rows + row) * waves, 8), waves)
            gathered[rows, :] = jnp.where(lane >= first, values, early[rows, :])

    def step(number, _):
        for inner in range(per_step):
            wave = number * per_step + inner
            column = gathered[pl.ds(wave, lat_total, stride=waves), :].astype(BF16)
            projected = lax.dot_general(
                legendre[wave], column, (((0,), (0,)), ((), ())), preferred_element_type=F32
            )
            staged[wave] = projected * factor[...]
            if (inner + 1) % per_copy == 0:
                rows = pl.ds(wave + 1 - per_copy, per_copy)
                pltpu.make_async_copy(staged.at[rows], out.at[rows], done).start()
        return 0

    lax.fori_loop(0, waves // per_step, step, 0)
    pltpu.make_async_copy(staged, out, done).wait()


VMEM = pl.BlockSpec(memory_space=pltpu.VMEM)
SMEM = pl.BlockSpec(memory_space=pltpu.SMEM)
ANY = pl.BlockSpec(memory_space=pl.ANY)


def limit(mib):
    return pltpu.CompilerParams(vmem_limit_bytes=mib * 2**20)


def cost(flops):
    return pl.CostEstimate(flops=flops, bytes_accessed=10**6, transcendentals=0)


def gathering(fields, req_block, req_stencil, req_frac, req_count, legendre):
    lat_rows, lon_cols, channels = fields.shape
    waves, lat_total, degrees = legendre.shape
    count, bands = lax.axis_size("lon"), lax.axis_size("lat")
    cells = lat_rows * lon_cols
    blocks = cells // BLK
    lon_total = lon_cols * count
    sector_waves = waves * bands
    chunks = chunk_list(channels)
    me = lax.axis_index("lon")
    here = jnp.stack([me, lax.axis_index("lat")]).astype(jnp.int32)

    table = hartley_constant(sector_waves * count, lon_total)
    table = lax.dynamic_slice_in_dim(table, me * sector_waves, sector_waves, axis=0)

    tile_rows = [blocks * BLK * width // LANES for _, width in chunks]
    tile_rows[0] += cells // LANES * 8
    packed = pl.pallas_call(
        functools.partial(pack_body, chunks, blocks),
        out_shape=[jax.ShapeDtypeStruct((rows, LANES), BF16) for rows in tile_rows],
        in_specs=[pl.BlockSpec(memory_space=pltpu.HBM)] * 5,
        out_specs=[VMEM] * len(tile_rows),
        scratch_shapes=[
            pltpu.VMEM((cells, channels), F32),
            pltpu.SMEM(req_count.shape[2:], jnp.int32),
            pltpu.VMEM((cells, channels), BF16),
            pltpu.VMEM(req_block.shape[2:], jnp.int32),
            pltpu.VMEM(req_stencil.shape[2:], jnp.int32),
            pltpu.VMEM(req_frac.shape[2:], jnp.int32),
            pltpu.SemaphoreType.DMA((5,)),
        ],
        compiler_params=limit(63),
        name="pack",
    )(req_count[0, 0], fields.reshape(cells, channels), req_block[0, 0], req_stencil[0, 0], req_frac[0, 0])

    near = [(i, i ^ step) for step in range(count) for i in range(count) if abs(i - (i ^ step)) <= count // 2]

    def after(tile, others):
        return lax.optimization_barrier((tile, *others))[0] if others else tile

    def exchange(tile, step, others=()):
        return lax.ppermute(after(tile, others), "lon", [pair for pair in near if pair[0] ^ pair[1] == step])

    def relay(tile, step):
        pairs = [(i ^ 1, i) for i in range(count) if (i, i ^ step) not in near]
        return lax.ppermute(tile, "lon", pairs)

    far = [step for step in range(count) if any((i, i ^ step) not in near for i in range(count))]
    parts = []
    params = ends = None
    ahead = moved = ()
    for number, (first, width) in enumerate(chunks):
        lead = number == 0
        tile = packed[number]
        near_tiles = {step: exchange(tile, step, ahead) for step in range(1, count) if step not in far}
        ahead = tuple(near_tiles.values())
        far_tiles = [(exchange(tile, step, ahead), step, True) for step in far]
        passed = [relay(near_tiles[step ^ 1], step) for step in far]
        far_tiles += [(got, step, False) for got, step in zip(passed, far, strict=True)]
        soon = [(tile, 0, True)] + [(got, step, True) for step, got in near_tiles.items()]
        last = soon + far_tiles if lead else far_tiles
        scratch = [
            pltpu.VMEM((count, BLK * width, blocks), BF16),
            pltpu.SMEM((count * SLOTS * (cells // SPAN + 1),), jnp.int32),
        ]
        grid = jax.ShapeDtypeStruct((lat_rows * width, lon_total), BF16)
        listed = [
            jax.ShapeDtypeStruct((count, cells // LANES * 8, LANES), BF16),
            jax.ShapeDtypeStruct((count, SLOTS + 1), jnp.int32),
        ]
        given = [] if lead else [params, ends]
        given_specs = [] if lead else [VMEM, SMEM]
        kept = [pltpu.VMEM(listed[0].shape, BF16), pltpu.SMEM(listed[1].shape, jnp.int32)]
        grid = pl.pallas_call(
            functools.partial(interp_body, count, bands, width, blocks, lead, False, far, [one[1:] for one in soon]),
            out_shape=grid,
            in_specs=[SMEM] + [VMEM] * len(soon) + given_specs,
            out_specs=VMEM,
            scratch_shapes=(kept if lead else []) + scratch,
            compiler_params=limit(24),
            cost_estimate=cost(width * 10**9),
            name="early",
        )(here, *[one[0] for one in soon], *given)
        ahead = (grid, *[got for got, _, _ in far_tiles])
        grid = after(grid, moved)
        results = pl.pallas_call(
            functools.partial(interp_body, count, bands, width, blocks, lead, True, far, [one[1:] for one in last]),
            out_shape=[jax.ShapeDtypeStruct((waves, lat_rows * width), BF16)] * bands
            + (listed if lead else []),
            in_specs=[SMEM] + [VMEM] * len(last) + given_specs + [VMEM, VMEM],
            out_specs=[VMEM] * bands + ([VMEM, SMEM] if lead else []),
            scratch_shapes=scratch
            + [
                pltpu.VMEM(grid.shape, BF16),
                pltpu.VMEM((sector_waves, lat_rows * width), BF16),
            ],
            compiler_params=limit(24),
            cost_estimate=cost(width * 5 * 10**7),
            name="late",
        )(here, *[one[0] for one in last], *given, grid, table)
        if lead:
            params, ends = results[bands:]
        pieces = [results[0]]
        for shift in range(1, bands):
            pieces.append(lax.ppermute(results[shift], "lat", [(i, i ^ shift) for i in range(bands)]))
        parts.append(pieces)
        moved = pieces[2:6]

    gathered = jax.ShapeDtypeStruct((lat_total * waves, channels), F32)
    early = [piece for pieces in parts[:-1] for piece in pieces]
    early = pl.pallas_call(
        functools.partial(collect_body, chunks[:-1], bands, lat_rows),
        out_shape=gathered,
        in_specs=[SMEM] + [VMEM] * len(early),
        out_specs=VMEM,
        compiler_params=limit(16),
        cost_estimate=cost(10**9),
        name="collect",
    )(here, *early)
    per_step = math.gcd(waves, 16)
    return pl.pallas_call(
        functools.partial(final_body, chunks[-1], bands, lat_rows, per_step, math.gcd(per_step, 4)),
        out_shape=jax.ShapeDtypeStruct((waves, degrees, channels), F32),
        in_specs=[SMEM] + [VMEM] * (bands + 2),
        out_specs=ANY,
        scratch_shapes=[
            pltpu.VMEM(gathered.shape, F32),
            pltpu.VMEM((degrees, channels), F32),
            pltpu.VMEM((waves, degrees, channels), F32),
            pltpu.SemaphoreType.DMA,
        ],
        compiler_params=limit(28),
        name="final",
    )(here, legendre, early, *parts[-1])


def padded(cells, sides, width):
    for axis, dim in sides:
        count = lax.axis_size(axis)
        head = lax.slice_in_dim(cells, 0, width, axis=dim)
        tail = lax.slice_in_dim(cells, cells.shape[dim] - width, cells.shape[dim], axis=dim)
        cells = jnp.concatenate(
            [
                lax.ppermute(tail, axis, [(i, (i + 1) % count) for i in range(count)]),
                cells,
                lax.ppermute(head, axis, [((i + 1) % count, i) for i in range(count)]),
            ],
            axis=dim,
        )
    return cells


def interpolate(own_tile, packed):
    cell_rows = packed[0][None, :] * BLK + packed[1:5]
    picked = jnp.take(own_tile, cell_rows.reshape(-1), axis=0).astype(F32)
    picked = picked.reshape(4, cell_rows.shape[1], own_tile.shape[1])
    frac_lat = (packed[5].astype(F32) + 0.5) / FRAC
    frac_lon = (packed[6].astype(F32) + 0.5) / FRAC
    weights = jnp.stack(
        [
            (1.0 - frac_lat) * (1.0 - frac_lon),
            frac_lat * (1.0 - frac_lon),
            (1.0 - frac_lat) * frac_lon,
            frac_lat * frac_lon,
        ]
    )
    return jnp.sum(weights[:, :, None] * picked, axis=0).astype(BF16)


def place_columns(values, counts, columns):
    slot_ends = jnp.cumsum(counts)
    starts = slot_ends - counts
    column = jnp.arange(columns, dtype=jnp.int32)
    slot_index = jnp.sum((slot_ends[None, :] <= column[:, None]).astype(jnp.int32), axis=1)
    onehot = slot_index[:, None] == jnp.arange(SLOTS, dtype=jnp.int32)[None, :]
    offset = column - jnp.sum(jnp.where(onehot, starts[None, :], 0), axis=1)
    flat_index = slot_index * values.shape[1] + offset
    return jnp.take(values.reshape(-1, values.shape[-1]), flat_index, axis=0)


def exchanging(fields, req_block, req_stencil, req_frac, req_count, legendre):
    lat_rows, lon_cols, channels = fields.shape
    count = lax.axis_size("lon")
    waves_total = legendre.shape[0] * count * lax.axis_size("lat")
    packed = jnp.concatenate(
        [req_block[0, 0][:, None, :], req_stencil[0, 0], req_frac[0, 0]], axis=1
    )
    counts = req_count[0, 0]
    widened = padded(fields, (("lon", 1),), lon_cols)
    slot_values = []
    for slot_index in range(SLOTS):
        owner_tile = widened[:, slot_index * lon_cols : (slot_index + 1) * lon_cols, :].reshape(
            -1, channels
        )
        slot_values.append(interpolate(owner_tile, packed[slot_index]))
    departed = place_columns(jnp.stack(slot_values), counts, lat_rows * lon_cols)
    departed = departed.reshape(lat_rows, lon_cols, channels)
    lon_total = lon_cols * count
    spectra = jnp.einsum(
        "kx,yxc->ykc",
        hartley_table(waves_total, lon_total),
        lax.all_to_all(departed, "lon", split_axis=0, concat_axis=1, tiled=True),
        preferred_element_type=F32,
    )
    fourier = lax.all_to_all(spectra.astype(BF16), "lon", split_axis=1, concat_axis=0, tiled=True)
    gathered = lax.all_to_all(fourier, "lat", split_axis=1, concat_axis=0, tiled=True)
    projected = jnp.einsum("kyn,ykc->knc", legendre, gathered, preferred_element_type=F32)
    degrees = legendre.shape[2]
    degree = jnp.arange(degrees, dtype=F32)
    factor = 1.0 / (1.0 + 4.0 * degree * (degree + 1.0) / (degrees * (degrees + 1)))
    return projected * factor[None, :, None]


def local(fields, req_block, req_stencil, req_frac, req_count, legendre):
    count = lax.axis_size("lon")
    lon_cols = fields.shape[1]
    sector_waves = legendre.shape[0] * lax.axis_size("lat")
    bands = lax.axis_size("lat")
    fits = count * lon_cols <= lon_cols + sector_waves
    fits = fits and bands & (bands - 1) == 0 and count & (count - 1) == 0
    plan = gathering if fits else exchanging
    return plan(fields, req_block, req_stencil, req_frac, req_count, legendre)


def solution(mesh):
    return jax.shard_map(
        local,
        mesh=mesh,
        in_specs=(
            P("lat", "lon", None),
            P("lat", "lon", None, None),
            P("lat", "lon", None, None, None),
            P("lat", "lon", None, None, None),
            P("lat", "lon", None),
            P(("lon", "lat"), None, None),
        ),
        out_specs=P(("lon", "lat"), None, None),
        check_vma=False,
    )
```
